32 devices in a mesh: grp: 2 (over y), var: 4 (over z), smp: 2 (over x), sub: 2 (over core).
Axes of the slice: x: 2, y: 2, z: 4, core: 2. Of those that a mesh axis runs over, the one named last changes fastest.
Arguments:
- dosages: int32 [2048, 8192], P('smp', ('grp', 'var', 'sub')), parts along dimension 1, may hold values from 0 to 200
- observed: int32 [2048, 8192], P('smp', ('grp', 'var', 'sub')), parts along dimension 1, may hold values from 0 to 1, as said below
Outputs:
- correlations: bfloat16 [8192, 4, 1024], P(('grp', 'var', 'smp'), None, 'sub'), parts along dimension 0
The draws below stay inside these ranges and needn't reach their ends.
There are 2 independent parts, one for each index of `grp`. The reference program is written for one: setup_inputs(seed, part) draws one part's arguments, and reference() takes and returns one part's arrays. A program takes and returns all parts, laid end to end along the dimension named above; each array names one. Nothing has to cross between parts.
Inputs may be any that keep to these rules, and one draw needn't show every extreme that they name: `observed`: each variant is missing in a share of samples of its own.
All inputs are finite; a program needn't handle non-finite values.
Results may differ from the reference program's by a relative error of at most 0.0051.
Values may be sent and summed in bfloat16 or wider, within the bound.
No kernel may reach another device: no remote copies, remote signals or barrier semaphores. Data moves between devices by JAX's collectives and lax.ppermute only.
A program may use at most 64 MiB of HBM per device.

```python
import math
import jax
import jax.numpy as jnp
from jax import lax

B = 1024
BAND = 4
S_DEV = 1024
SAMPLES = 2048
VARIANTS = 4096
N_SMP = 2


def draw_dosages(key, part):
    keys = jax.random.split(jax.random.fold_in(key, 11), 4)
    rows_all = SAMPLES
    cols_all = VARIANTS
    window = BAND * B
    base_code = jax.random.randint(keys[0], (1, cols_all), 30, 130)
    direction = jax.random.randint(keys[1], (1, cols_all), 0, 2) * 2 - 1
    positions = jnp.arange(rows_all, dtype=jnp.int32)[:, None]
    strata = (2 * positions - rows_all) * 60 // rows_all * direction
    steps_all = jax.random.randint(keys[2], (rows_all, cols_all + window), -1, 2)
    running = jnp.concatenate([jnp.zeros((rows_all, 1), jnp.int32), jnp.cumsum(steps_all, axis=1)], axis=1)
    windowed = running[:, window:window + cols_all] - running[:, 0:cols_all]
    divisor = max(1, int(math.sqrt(window * 2 / 3)))
    latent = windowed * 40 // divisor
    noise_part = jax.random.randint(keys[3], (rows_all, cols_all), -40, 41)
    return jnp.clip(base_code + strata + latent + noise_part, 0, 200).astype(jnp.int32)


def draw_observed(key, part):
    keys = jax.random.split(jax.random.fold_in(key, 23), 2)
    missing = jax.random.randint(keys[0], (1, VARIANTS), 1, 40)
    tickets = jax.random.randint(keys[1], (SAMPLES, VARIANTS), 0, 100)
    return (tickets >= missing).astype(jnp.int32)


def setup_inputs(seed: int = 0, part: int = 0) -> dict:
    key_list = jax.random.split(jax.random.key(seed), 3)
    part_splits = jax.random.split(jax.random.fold_in(key_list[2], part), 3)
    return {
        "dosages": draw_dosages(jax.random.fold_in(jax.random.fold_in(key_list[2], part), 71), part),
        "observed": draw_observed(jax.random.fold_in(jax.random.fold_in(key_list[2], part), 71), part),
    }


def reference(dosages, observed):
    values = dosages.astype(jnp.float32) / 100.0
    weights = observed.astype(jnp.float32)
    counts = jnp.maximum(lax.optimization_barrier(jnp.sum(weights, axis=0)), 1.0)
    means = lax.optimization_barrier(jnp.sum(weights * values, axis=0)) / counts
    centered = values - means
    spreads = lax.optimization_barrier(jnp.sum(weights * centered * centered, axis=0)) / counts
    standard = (weights * centered * lax.rsqrt(spreads + 1e-05)).astype(jnp.bfloat16)
    samples = standard.shape[0]
    blocks = standard.shape[1] // B
    padded = jnp.concatenate([standard, jnp.zeros((samples, (BAND - 1) * B), jnp.bfloat16)], axis=1)

    def one_block(block_index):
        begin = (block_index * B).astype(jnp.int32)
        rows_part = lax.dynamic_slice_in_dim(padded, begin, B, 1).astype(jnp.float32).reshape(N_SMP, S_DEV, B)
        band_part = lax.dynamic_slice_in_dim(padded, begin, BAND * B, 1).astype(jnp.float32).reshape(N_SMP, S_DEV, BAND * B)
        partial_sums = jnp.einsum('psr,psc->prc', rows_part, band_part, precision=lax.Precision.HIGHEST) / samples
        rounded = lax.optimization_barrier(partial_sums.astype(jnp.bfloat16)).astype(jnp.float32)
        summed = lax.optimization_barrier(jnp.sum(rounded, axis=0)).astype(jnp.bfloat16)
        return summed.reshape(B, BAND, B)
    result = lax.map(one_block, jnp.arange(blocks, dtype=jnp.int32))
    return result.reshape(blocks * B, BAND, B)
```

```python
import jax
import jax.numpy as jnp
from jax import lax
from jax.sharding import PartitionSpec as P

BAND = 4
CHUNKS = 2


def shifted(block, axis, distance):
    devices = range(lax.axis_size(axis))
    route = [(i - distance, i) for i in devices if i - distance in devices]
    return lax.ppermute(block, axis, route)


def rotated(block, axis, distance):
    n = lax.axis_size(axis)
    return lax.ppermute(block, axis, [(i, (i + distance) % n) for i in range(n)])


def standardize(code, stats):
    value = code.astype(jnp.float32)
    return jnp.where(value >= 0, (value - stats[0:1]) * stats[1:2], 0.0).astype(jnp.bfloat16)


def variant_stats(sums):
    counts = jnp.maximum(sums[0], 1)
    n = counts.astype(jnp.float32)
    pivot = jnp.round(sums[1].astype(jnp.float32) / n).astype(jnp.int32)
    rest = (sums[1] - pivot * counts).astype(jnp.float32)
    squares = (sums[2] - 2 * pivot * sums[1] + pivot * pivot * sums[0]).astype(jnp.float32)
    spreads = (squares - rest * rest / n) / n * 1e-4
    means = pivot.astype(jnp.float32) + rest / n
    return jnp.stack([means, lax.rsqrt(spreads + 1e-05) * 0.01])


def on_device(dosages, observed):
    n_smp = lax.axis_size("smp")
    n_sub = lax.axis_size("sub")
    me_smp = lax.axis_index("smp")
    me_sub = lax.axis_index("sub")
    samples, width = dosages.shape
    rows_owned = width * n_sub // n_smp
    factor = 1.0 / (samples * n_smp)

    kept = observed > 0
    code = jnp.where(kept, dosages, -1).astype(jnp.bfloat16)
    known = jnp.where(kept, dosages, 0)
    sums_own = jnp.stack(
        [jnp.sum(observed, axis=0), jnp.sum(known, axis=0), jnp.sum(known * known, axis=0)]
    )
    sums = sums_own
    for d in range(1, n_smp):
        sums = sums + rotated(sums_own, "smp", d)
    stats = variant_stats(sums)

    piece = width // CHUNKS
    chunks = [lax.slice_in_dim(code, c * piece, (c + 1) * piece, axis=1) for c in range(CHUNKS)]
    codes = [chunks]
    for _ in range(1, BAND):
        codes.append([shifted(x, "var", -1) for x in codes[-1]])
    all_stats = [stats] + [shifted(stats, "var", -k) for k in range(1, BAND)]

    own = standardize(code, stats)
    parts = [own] + [rotated(own, "sub", d) for d in range(1, n_sub)]
    whole = jnp.zeros((samples, n_sub * width), jnp.bfloat16)
    for d, part in enumerate(parts):
        whole = lax.dynamic_update_slice_in_dim(whole, part, (me_sub - d) % n_sub * width, 1)
    rows = [
        lax.dynamic_slice_in_dim(whole, (me_smp + d) % n_smp * rows_owned, rows_owned, 1)
        for d in range(n_smp)
    ]

    def product(left, right):
        out = lax.dot_general(
            left, right, (((0,), (0,)), ((), ())), preferred_element_type=jnp.float32
        )
        return (out * factor).astype(jnp.bfloat16)

    panels = []
    for k in range(BAND):
        cols = [
            standardize(codes[k][c], all_stats[k][:, c * piece:(c + 1) * piece])
            for c in range(CHUNKS)
        ]
        for c in range(CHUNKS):
            total = product(rows[0], cols[c]).astype(jnp.float32)
            for d in range(1, n_smp):
                total = total + rotated(product(rows[d], cols[c]), "smp", d).astype(jnp.float32)
            panels.append(total.astype(jnp.bfloat16))
    return jnp.concatenate(panels, axis=1).reshape(rows_owned, BAND, width)


def solution(mesh):
    in_specs = (P("smp", ("grp", "var", "sub")), P("smp", ("grp", "var", "sub")))
    out_specs = P(("grp", "var", "smp"), None, "sub")
    return jax.shard_map(
        on_device, mesh=mesh, in_specs=in_specs, out_specs=out_specs, check_vma=False
    )
```

```python
import functools

import jax
import jax.numpy as jnp
from jax import lax
from jax.experimental import pallas as pl
from jax.experimental.pallas import tpu as pltpu
from jax.sharding import PartitionSpec as P

BAND = 4
TAIL = 16


def params(mib):
    return pltpu.CompilerParams(vmem_limit_bytes=mib * 1024 * 1024)


def split3(x):
    high = x.astype(jnp.bfloat16)
    rest = x - high.astype(jnp.float32)
    middle = rest.astype(jnp.bfloat16)
    low = (rest - middle.astype(jnp.float32)).astype(jnp.bfloat16)
    return [high, middle, low]


def encode_body(dosages, observed, first, second, sums, held_d, held_o, sems):
    steps = sems.shape[1]
    samples, width = held_d.shape
    rows = samples // steps
    spans = [pl.ds(i * rows, rows) for i in range(steps)]
    copies = [
        [
            pltpu.make_async_copy(src.at[span], dst.at[span], sems.at[j, i])
            for j, (src, dst) in enumerate(((dosages, held_d), (observed, held_o)))
        ]
        for i, span in enumerate(spans)
    ]
    for pair in copies:
        for copy in pair:
            copy.start()
    parts = [jnp.zeros((8, width), jnp.int32)] * 3
    for span, pair in zip(spans, copies):
        for copy in pair:
            copy.wait()
        weights = held_o[span]
        known = held_d[span] * weights
        code = (known + (weights - 1)).astype(jnp.float32).astype(jnp.bfloat16)
        first[span] = code[:, :first.shape[1]]
        second[span] = code[:, first.shape[1]:]
        for i, part in enumerate((weights, known, known * known)):
            parts[i] += jnp.sum(part.reshape(rows // 8, 8, width), axis=0)
    rows_out = [jnp.sum(p, axis=0, keepdims=True) for p in parts]
    sums[...] = jnp.concatenate(rows_out + [jnp.zeros((5, width), jnp.int32)], axis=0)


def call(body, name, shapes, inputs, mib=32, in_hbm=False, scratch=(), events=()):
    place = pltpu.HBM if in_hbm else pltpu.VMEM
    n = len(inputs)
    skip = len(events)

    def with_events(*refs):
        body(*refs[:n], *refs[n + skip:])

    return pl.pallas_call(
        with_events,
        in_specs=[pl.BlockSpec(memory_space=place)] * n
        + [pl.BlockSpec(memory_space=pl.ANY)] * skip,
        out_specs=[pl.BlockSpec(memory_space=pltpu.VMEM)] * len(shapes),
        out_shape=[jax.ShapeDtypeStruct(shape, kind) for shape, kind in shapes],
        scratch_shapes=scratch,
        compiler_params=params(mib),
        cost_estimate=pl.CostEstimate(flops=0, bytes_accessed=0, transcendentals=0),
        name=name,
    )(*inputs, *events)


def encode(dosages, observed):
    samples, width = dosages.shape
    steps = 8
    cut = width // 4
    return call(
        encode_body,
        "encode",
        [
            ((samples, cut), jnp.bfloat16),
            ((samples, width - cut), jnp.bfloat16),
            ((8, width), jnp.int32),
        ],
        [dosages, observed],
        in_hbm=True,
        scratch=[
            pltpu.VMEM((samples, width), jnp.int32),
            pltpu.VMEM((samples, width), jnp.int32),
            pltpu.SemaphoreType.DMA((2, steps)),
        ],
    )


def variant_stats(sums):
    counts = jnp.maximum(sums[0], 1)
    n = counts.astype(jnp.float32)
    pivot = jnp.floor(sums[1].astype(jnp.float32) / n + 0.5).astype(jnp.int32)
    rest = (sums[1] - pivot * counts).astype(jnp.float32)
    squares = (sums[2] - 2 * pivot * sums[1] + pivot * pivot * sums[0]).astype(jnp.float32)
    spreads = (squares - rest * rest / n) / n * 1e-4
    means = pivot.astype(jnp.float32) + rest / n
    return means, lax.rsqrt(spreads + 1e-05) * 0.01


def standardize(code, means, scales):
    value = code.astype(jnp.float32)
    return jnp.where(value >= 0, (value - means) * scales, 0.0).astype(jnp.bfloat16)


def finish_body(first, second, *refs):
    sums_refs, (own, for_up, for_down, last) = refs[:-4], refs[-4:]
    samples, cut = first.shape
    width = own.shape[1]
    sums = [sum(r[i:i + 1] for r in sums_refs) for i in range(3)]
    means, scales = variant_stats(sums)
    own[:, :cut] = standardize(first[...], means[:, :cut], scales[:, :cut])
    rest = standardize(second[...], means[:, cut:], scales[:, cut:])
    own[:, cut:] = rest
    for_up[:samples] = rest
    middle = for_down.shape[1]
    for_down[:samples] = rest[:, :middle]
    last[...] = rest[:, middle:]
    rows = split3(means[:, :cut]) + split3(scales[:, :cut])
    tail = jnp.concatenate(rows + [jnp.zeros((TAIL - len(rows), cut), jnp.bfloat16)], axis=0)
    for ref in (for_up, for_down):
        ref[samples:, :cut] = tail
        ref[samples:, cut:] = jnp.zeros((TAIL, ref.shape[1] - cut), jnp.bfloat16)


def finish(first, second, all_sums, events):
    samples, cut = first.shape
    rest = second.shape[1]
    shapes = [
        (samples, cut + rest),
        (samples + TAIL, rest),
        (samples + TAIL, rest - cut),
        (samples, cut),
    ]
    return call(
        finish_body,
        "finish",
        [(s, jnp.bfloat16) for s in shapes],
        [first, second, *all_sums],
        events=events,
    )


def interleave_body(*refs):
    out = refs[-1]
    for k in range(BAND):
        out[:, k, :] = refs[k][...]


def interleave(panels):
    rows, width = panels[0].shape
    tile = min(rows, 128)
    return pl.pallas_call(
        interleave_body,
        grid=(rows // tile,),
        in_specs=[pl.BlockSpec((tile, width), lambda i: (i, 0))] * BAND,
        out_specs=pl.BlockSpec((tile, BAND, width), lambda i: (i, 0, 0)),
        out_shape=jax.ShapeDtypeStruct((rows, BAND, width), jnp.bfloat16),
        compiler_params=params(32),
        name="interleave",
    )(*panels)


def product(whole, cols, distance):
    n_smp = lax.axis_size("smp")
    owned = whole.shape[1] // n_smp
    place = lax.rem(lax.axis_index("smp") + distance, n_smp)
    left = whole[:, pl.ds(pl.multiple_of(place * owned, owned), owned)]
    out = lax.dot_general(left, cols, (((0,), (0,)), ((), ())), preferred_element_type=jnp.float32)
    return out * (1.0 / (whole.shape[0] * n_smp))


def send_parts(whole, cols, parts):
    for d, ref in enumerate(parts):
        ref[...] = product(whole, cols, d + 1).astype(jnp.bfloat16)


def gather_body(n_sub, *refs):
    held, cols, whole, parts = refs[:n_sub], refs[n_sub], refs[n_sub + 1], refs[n_sub + 2:]
    width = held[0].shape[1]
    me = lax.axis_index("sub")
    for d in range(n_sub):
        place = lax.rem(me - d + n_sub, n_sub)
        whole[:, pl.ds(pl.multiple_of(place * width, width), width)] = held[d][...]
    send_parts(whole, cols[...], parts)


def from_tail(message, samples, cut):
    rows = [message[samples + i:samples + i + 1, :cut].astype(jnp.float32) for i in range(6)]
    return (rows[0] + rows[1]) + rows[2], (rows[3] + rows[4]) + rows[5]


def assemble_body(first, message, *refs):
    *rest, out = refs
    samples, cut = first.shape
    end = message.shape[1] + cut
    out[:, :cut] = standardize(first[...], *from_tail(message, samples, cut))
    out[:, cut:end] = message[:samples]
    for ref in rest:
        out[:, end:end + ref.shape[1]] = ref[...]
        end += ref.shape[1]


def cols_body(n_in, whole, *refs):
    pieces, cols, parts = refs[:n_in], refs[n_in], refs[n_in + 1:]
    assemble_body(*pieces, cols)
    send_parts(whole, cols[...], parts)


def plain_body(whole, cols, *parts):
    send_parts(whole, cols[...], parts)


def total_body(whole, cols, *refs):
    *arrived, out = refs
    total = product(whole, cols[...], 0).astype(jnp.bfloat16).astype(jnp.float32)
    for ref in arrived:
        total = total + ref[...].astype(jnp.float32)
    out[...] = total.astype(jnp.bfloat16)


def fence_body(*refs):
    refs[-1][...] = jnp.zeros_like(refs[-1])


def fence(*events):
    return pl.pallas_call(
        fence_body,
        in_specs=[pl.BlockSpec(memory_space=pl.ANY)] * len(events),
        out_specs=pl.BlockSpec(memory_space=pltpu.VMEM),
        out_shape=jax.ShapeDtypeStruct((8, 128), jnp.float32),
        compiler_params=params(1),
        cost_estimate=pl.CostEstimate(flops=2 * 10**10, bytes_accessed=0, transcendentals=0),
        name="fence",
    )(*events)


def together(*arrays):
    return lax.optimization_barrier(arrays)


def on_device(dosages, observed):
    n_var = lax.axis_size("var")
    n_smp = lax.axis_size("smp")
    n_sub = lax.axis_size("sub")
    samples, width = dosages.shape
    rows_owned = width * n_sub // n_smp

    def along(x, distance, keep):
        route = [
            (i, i + distance) for i in range(n_var) if 0 <= i + distance < n_var and keep(i)
        ]
        return lax.ppermute(x, "var", route)

    def down(x):
        return along(x, -1, lambda i: True)

    def down_again(x):
        return along(x, -1, lambda i: i + 1 < n_var)

    def up_two(x):
        return along(x, 2, lambda i: i + 3 < n_var)

    def holds_three(i):
        return i >= 2 and i + 1 < n_var

    def down_two(x):
        return along(x, -2, holds_three)

    def swapped(x, axis, distance, keep=None):
        n = lax.axis_size(axis)
        if keep is None:
            return lax.ppermute(x, axis, [(i, (i + distance) % n) for i in range(n)])
        route = [
            (v * n + i, v * n + (i + distance) % n)
            for v in range(n_var)
            if keep(v)
            for i in range(n)
        ]
        return lax.ppermute(x, ("var", axis), route)

    def others_of(part):
        return [swapped(part, "sub", d) for d in range(1, n_sub)]

    def sent(parts, keep=None):
        return [swapped(p, "smp", d + 1, keep) for d, p in enumerate(parts)]

    def part_shapes(columns):
        return [((rows_owned, columns), jnp.bfloat16)] * (n_smp - 1)

    def gather(part, others, cols, name, events):
        block = ((samples, width * n_sub), jnp.bfloat16)
        body = functools.partial(gather_body, n_sub)
        shapes = [block] + part_shapes(width)
        whole, *parts = call(body, name, shapes, [part, *others, cols], events=events)
        return whole, parts

    def columns(whole, pieces, name, events):
        span = sum(p.shape[1] for p in pieces)
        body = functools.partial(cols_body, len(pieces))
        shapes = [((samples, span), jnp.bfloat16)] + part_shapes(span)
        cols, *parts = call(body, name, shapes, [whole, *pieces], events=events)
        return cols, parts

    def total(whole, cols, arrived, name, events):
        shape = ((rows_owned, cols.shape[1]), jnp.bfloat16)
        return call(total_body, name, [shape], [whole, cols, *arrived], events=events)[0]

    cut = width // 4

    first, second, sums_own = encode(dosages, observed)
    near_a, up_a = down(first), up_two(first)
    arrived_sums = [swapped(sums_own, "smp", d) for d in range(1, n_smp)]
    step = fence(first)
    own, for_up, for_down, last = finish(first, second, [sums_own] + arrived_sums, [step])
    near_b, up_b = down(for_down), up_two(for_up)
    others = others_of(own)
    step = fence(own)

    whole, part0 = gather(own, others, own, "gather0", [near_a, up_a, step])
    last, near_a, *part0 = together(last, near_a, *part0)
    near_c = down(last)
    far_a = down_again(near_a)
    got0 = sent(part0)
    step = fence(whole, *part0)
    near_b, step = together(near_b, step)
    far_b = down_again(near_b)
    step = fence(near_b, step)
    near_c, step = together(near_c, step)
    far_c = down_again(near_c)

    (rows3,) = call(
        assemble_body,
        "rows3",
        [((samples, width), jnp.bfloat16)],
        [up_a, up_b],
        events=[near_c, step],
    )
    others3 = others_of(rows3)
    step = fence(rows3)
    cols1, part1 = columns(whole, [near_a, near_b, near_c], "columns1", [step, *got0])
    got1 = sent(part1, lambda v: not holds_three(v) and v + 1 < n_var)
    step = fence(cols1)
    panel0 = total(whole, own, got0, "total0", [step])
    whole3, part3 = gather(rows3, others3, cols1, "gather3", [panel0])
    got3 = sent(part3, holds_three)
    *part1, far_a, whole3 = together(*part1, far_a, whole3)
    got1_late = sent(part1, holds_three)
    step = fence(far_a, whole3)

    cols2, part2 = columns(whole, [far_a, far_b], "columns2", [step, *got1])
    got2 = sent(part2, lambda v: v + 2 < n_var)
    step = fence(cols2)
    panel3 = total(whole3, cols1, got3, "total3", [step])
    step = fence(panel3)
    panel3 = down_two(panel3)
    part2_c = call(plain_body, "last2", part_shapes(cut), [whole, far_c], events=[step])
    got2_c = sent(part2_c, lambda v: v + 2 < n_var)
    step = fence(*part2_c)
    panel2_ab = total(whole, cols2, got2, "total2", [step])
    panel2_c = total(whole, far_c, got2_c, "total2c", [panel2_ab])
    panel1 = total(whole, cols1, got1 + got1_late, "total1", [panel2_c])
    panel2 = jnp.concatenate([panel2_ab, panel2_c], axis=1)
    return interleave([panel0, panel1, panel2, panel3])


def solution(mesh):
    in_specs = (P("smp", ("grp", "var", "sub")), P("smp", ("grp", "var", "sub")))
    out_specs = P(("grp", "var", "smp"), None, "sub")
    return jax.shard_map(
        on_device, mesh=mesh, in_specs=in_specs, out_specs=out_specs, check_vma=False
    )
```

```python
import functools

import jax
import jax.numpy as jnp
from jax import lax
from jax.experimental import pallas as pl
from jax.experimental.pallas import tpu as pltpu
from jax.sharding import PartitionSpec as P

BAND = 4
TAIL = 16


def params(mib):
    return pltpu.CompilerParams(vmem_limit_bytes=mib * 1024 * 1024)


def split3(x):
    high = x.astype(jnp.bfloat16)
    rest = x - high.astype(jnp.float32)
    middle = rest.astype(jnp.bfloat16)
    low = (rest - middle.astype(jnp.float32)).astype(jnp.bfloat16)
    return [high, middle, low]


def encode_body(dosages, observed, first, second, sums, held_d, held_o, sems):
    steps = sems.shape[1]
    samples, width = held_d.shape
    rows = samples // steps
    spans = [pl.ds(i * rows, rows) for i in range(steps)]
    copies = [
        [
            pltpu.make_async_copy(src.at[span], dst.at[span], sems.at[j, i])
            for j, (src, dst) in enumerate(((dosages, held_d), (observed, held_o)))
        ]
        for i, span in enumerate(spans)
    ]
    for pair in copies:
        for copy in pair:
            copy.start()
    parts = [jnp.zeros((8, width), jnp.int32)] * 3
    for span, pair in zip(spans, copies):
        for copy in pair:
            copy.wait()
        weights = held_o[span]
        known = held_d[span] * weights
        code = (known + (weights - 1)).astype(jnp.float32).astype(jnp.bfloat16)
        first[span] = code[:, :first.shape[1]]
        second[span] = code[:, first.shape[1]:]
        for i, part in enumerate((weights, known, known * known)):
            parts[i] += jnp.sum(part.reshape(rows // 8, 8, width), axis=0)
    rows_out = [jnp.sum(p, axis=0, keepdims=True) for p in parts]
    sums[...] = jnp.concatenate(rows_out + [jnp.zeros((5, width), jnp.int32)], axis=0)


def call(body, name, shapes, inputs, mib=32, in_hbm=False, scratch=(), events=()):
    place = pltpu.HBM if in_hbm else pltpu.VMEM
    n = len(inputs)
    skip = len(events)

    def with_events(*refs):
        body(*refs[:n], *refs[n + skip:])

    return pl.pallas_call(
        with_events,
        in_specs=[pl.BlockSpec(memory_space=place)] * n
        + [pl.BlockSpec(memory_space=pl.ANY)] * skip,
        out_specs=[pl.BlockSpec(memory_space=pltpu.VMEM)] * len(shapes),
        out_shape=[jax.ShapeDtypeStruct(shape, kind) for shape, kind in shapes],
        scratch_shapes=scratch,
        compiler_params=params(mib),
        cost_estimate=pl.CostEstimate(flops=0, bytes_accessed=0, transcendentals=0),
        name=name,
    )(*inputs, *events)


def encode(dosages, observed):
    samples, width = dosages.shape
    steps = 8
    cut = width // 2
    return call(
        encode_body,
        "encode",
        [
            ((samples, cut), jnp.bfloat16),
            ((samples, width - cut), jnp.bfloat16),
            ((8, width), jnp.int32),
        ],
        [dosages, observed],
        in_hbm=True,
        scratch=[
            pltpu.VMEM((samples, width), jnp.int32),
            pltpu.VMEM((samples, width), jnp.int32),
            pltpu.SemaphoreType.DMA((2, steps)),
        ],
    )


def variant_stats(sums):
    counts = jnp.maximum(sums[0], 1)
    n = counts.astype(jnp.float32)
    pivot = jnp.floor(sums[1].astype(jnp.float32) / n + 0.5).astype(jnp.int32)
    rest = (sums[1] - pivot * counts).astype(jnp.float32)
    squares = (sums[2] - 2 * pivot * sums[1] + pivot * pivot * sums[0]).astype(jnp.float32)
    spreads = (squares - rest * rest / n) / n * 1e-4
    means = pivot.astype(jnp.float32) + rest / n
    return means, lax.rsqrt(spreads + 1e-05) * 0.01


def standardize(code, means, scales):
    value = code.astype(jnp.float32)
    return jnp.where(value >= 0, (value - means) * scales, 0.0).astype(jnp.bfloat16)


def finish_body(first, second, *refs):
    sums_refs, (own, message) = refs[:-2], refs[-2:]
    samples, cut = first.shape
    sums = [sum(r[i:i + 1] for r in sums_refs) for i in range(3)]
    means, scales = variant_stats(sums)
    own[:, :cut] = standardize(first[...], means[:, :cut], scales[:, :cut])
    rest = standardize(second[...], means[:, cut:], scales[:, cut:])
    own[:, cut:] = rest
    message[:samples] = rest
    rows = split3(means[:, :cut]) + split3(scales[:, :cut])
    rows.append(jnp.zeros((TAIL - len(rows), cut), jnp.bfloat16))
    message[samples:] = jnp.concatenate(rows, axis=0)


def finish(first, second, all_sums, events):
    samples, cut = first.shape
    return call(
        finish_body,
        "finish",
        [((samples, 2 * cut), jnp.bfloat16), ((samples + TAIL, cut), jnp.bfloat16)],
        [first, second, *all_sums],
        events=events,
    )


def interleave_body(first, second, third_a, third_b, fourth, out):
    cut = third_a.shape[1]
    out[:, 0, :] = first[...]
    out[:, 1, :] = second[...]
    out[:, 2, :cut] = third_a[...]
    out[:, 2, cut:] = third_b[...]
    out[:, 3, :] = fourth[...]


def interleave(panels):
    rows, width = panels[0].shape
    tile = min(rows, 128)
    return pl.pallas_call(
        interleave_body,
        grid=(rows // tile,),
        in_specs=[pl.BlockSpec((tile, p.shape[1]), lambda i: (i, 0)) for p in panels],
        out_specs=pl.BlockSpec((tile, BAND, width), lambda i: (i, 0, 0)),
        out_shape=jax.ShapeDtypeStruct((rows, BAND, width), jnp.bfloat16),
        compiler_params=params(32),
        name="interleave",
    )(*panels)


def product(whole, cols, distance):
    n_smp = lax.axis_size("smp")
    owned = whole.shape[1] // n_smp
    place = lax.rem(lax.axis_index("smp") + distance, n_smp)
    left = whole[:, pl.ds(pl.multiple_of(place * owned, owned), owned)]
    out = lax.dot_general(left, cols, (((0,), (0,)), ((), ())), preferred_element_type=jnp.float32)
    return out * (1.0 / (whole.shape[0] * n_smp))


def send_parts(whole, cols, parts):
    for d, ref in enumerate(parts):
        ref[...] = product(whole, cols, d + 1).astype(jnp.bfloat16)


def gather_body(n_sub, n_held, *refs):
    held, cols, whole, parts = refs[:n_held], refs[n_held], refs[n_held + 1], refs[n_held + 2:]
    width = held[0].shape[1]
    pieces = (n_held - 1) // (n_sub - 1)
    count = whole.shape[0] // pieces
    me = lax.axis_index("sub")

    def span(d):
        place = lax.rem(me - d + n_sub, n_sub)
        return pl.ds(pl.multiple_of(place * width, width), width)

    whole[:, span(0)] = held[0][...]
    for d in range(1, n_sub):
        for i in range(pieces):
            whole[i * count:(i + 1) * count, span(d)] = held[1 + (d - 1) * pieces + i][...]
    send_parts(whole, cols[...], parts)


def from_tail(tail):
    rows = [tail[i:i + 1].astype(jnp.float32) for i in range(6)]
    return (rows[0] + rows[1]) + rows[2], (rows[3] + rows[4]) + rows[5]


def assemble_body(first, message, out):
    samples, cut = first.shape
    out[:, :cut] = standardize(first[...], *from_tail(message[samples:]))
    out[:, cut:] = message[:samples]


def near_body(whole, first, message, cols, half, *parts):
    assemble_body(first, message, cols)
    half[...] = cols[:, :half.shape[1]]
    send_parts(whole, cols[...], parts)


def far_body(whole, cols, *parts):
    send_parts(whole, cols[:whole.shape[0]], parts)


def total_body(whole, cols, *refs):
    *arrived, out = refs
    total = product(whole, cols[:whole.shape[0]], 0).astype(jnp.bfloat16).astype(jnp.float32)
    for ref in arrived:
        total = total + ref[...].astype(jnp.float32)
    out[...] = total.astype(jnp.bfloat16)


def fence_body(*refs):
    refs[-1][...] = jnp.zeros_like(refs[-1])


def fence(weight, *events):
    return pl.pallas_call(
        fence_body,
        in_specs=[pl.BlockSpec(memory_space=pl.ANY)] * len(events),
        out_specs=pl.BlockSpec(memory_space=pltpu.VMEM),
        out_shape=jax.ShapeDtypeStruct((8, 128), jnp.float32),
        compiler_params=params(1),
        cost_estimate=pl.CostEstimate(flops=weight * 10**9, bytes_accessed=0, transcendentals=0),
        name="fence",
    )(*events)


def together(*arrays):
    return lax.optimization_barrier(arrays)


def on_device(dosages, observed):
    n_var = lax.axis_size("var")
    n_smp = lax.axis_size("smp")
    n_sub = lax.axis_size("sub")
    samples, width = dosages.shape
    rows_owned = width * n_sub // n_smp

    def along(x, distance, keep):
        route = [
            (i, i + distance) for i in range(n_var) if 0 <= i + distance < n_var and keep(i)
        ]
        return lax.ppermute(x, "var", route)

    def down(x):
        return along(x, -1, lambda i: True)

    def down_again(x):
        return along(x, -1, lambda i: i + 1 < n_var)

    def up_two(x):
        return along(x, 2, lambda i: i + 3 < n_var)

    def holds_three(i):
        return i >= 2 and i + 1 < n_var

    def down_two(x):
        return along(x, -2, holds_three)

    def swapped(x, axis, distance, keep=None):
        n = lax.axis_size(axis)
        if keep is None:
            return lax.ppermute(x, axis, [(i, (i + distance) % n) for i in range(n)])
        route = [
            (v * n + i, v * n + (i + distance) % n)
            for v in range(n_var)
            if keep(v)
            for i in range(n)
        ]
        return lax.ppermute(x, ("var", axis), route)

    def others_of(part, pieces):
        count = part.shape[0] // pieces
        cuts = [part[i * count:(i + 1) * count] for i in range(pieces)]
        return [swapped(c, "sub", d) for d in range(1, n_sub) for c in cuts]

    def sent(parts, keep=None):
        return [swapped(p, "smp", d + 1, keep) for d, p in enumerate(parts)]

    def part_shapes(columns):
        return [((rows_owned, columns), jnp.bfloat16)] * (n_smp - 1)

    def gather(part, others, cols, name, events):
        block = ((samples, width * n_sub), jnp.bfloat16)
        body = functools.partial(gather_body, n_sub, 1 + len(others))
        shapes = [block] + part_shapes(width)
        whole, *parts = call(body, name, shapes, [part, *others, cols], events=events)
        return whole, parts

    def total(whole, cols, arrived, name, events):
        shape = ((rows_owned, cols.shape[1]), jnp.bfloat16)
        return call(total_body, name, [shape], [whole, cols, *arrived], events=events)[0]

    first, second, sums_own = encode(dosages, observed)
    near_a = down(first)
    step = fence(20, first)
    sums_own, first_up, step = together(sums_own, first, step)
    up_a = up_two(first_up)
    arrived_sums = [swapped(sums_own, "smp", d) for d in range(1, n_smp)]
    step = fence(20, step)
    own, message = finish(first, second, [sums_own] + arrived_sums, [step])
    near_b, up_b = down(message), up_two(message)
    others = others_of(own, 1)
    step = fence(20, own)

    whole, part0 = gather(own, others, own, "gather0", [near_a, step])
    got0 = sent(part0)
    near_b, whole = together(near_b, whole)
    far_b = down_again(near_b)
    half = ((samples, width // 2), jnp.bfloat16)
    cols1, near_a, *part1 = call(
        near_body,
        "near",
        [((samples, width), jnp.bfloat16), half] + part_shapes(width),
        [whole, near_a, near_b],
    )
    far_a = down_again(near_a)
    (rows3,) = call(
        assemble_body,
        "rows3",
        [((samples, width), jnp.bfloat16)],
        [up_a, up_b],
        events=[cols1],
    )
    others3 = others_of(rows3, 2)
    panel0 = total(whole, own, got0, "total0", [rows3])
    whole3, part3 = gather(rows3, others3, cols1, "gather3", [fence(3, panel0)])
    got3 = sent(part3, holds_three)
    part2_b = call(far_body, "far_b", part_shapes(width // 2), [whole, far_b], events=[whole3])
    got2_b = sent(part2_b)
    step = fence(12, *part2_b)
    panel3 = total(whole3, cols1, got3, "total3", [step])
    *part1, panel3 = together(*part1, panel3)
    got1 = sent(part1)
    panel3 = down_two(panel3)
    part2_a = call(
        far_body, "far_a", part_shapes(width // 2), [whole, far_a], events=[*part1]
    )
    got2_a = sent(part2_a, lambda v: v + 2 < n_var)
    panel2_b = total(whole, far_b, got2_b, "total2b", [*part2_a])
    step = fence(3, panel2_b)
    panel1 = total(whole, cols1, got1, "total1", [step])
    panel2_a = total(whole, far_a, got2_a, "total2a", [panel1])
    return interleave([panel0, panel1, panel2_a, panel2_b, panel3])


def solution(mesh):
    in_specs = (P("smp", ("grp", "var", "sub")), P("smp", ("grp", "var", "sub")))
    out_specs = P(("grp", "var", "smp"), None, "sub")
    return jax.shard_map(
        on_device, mesh=mesh, in_specs=in_specs, out_specs=out_specs, check_vma=False
    )
```

```python
import functools

import jax
import jax.numpy as jnp
from jax import lax
from jax.experimental import pallas as pl
from jax.experimental.pallas import tpu as pltpu
from jax.sharding import PartitionSpec as P

BAND = 4
TAIL = 16


def params(mib):
    return pltpu.CompilerParams(vmem_limit_bytes=mib * 1024 * 1024)


def split3(x):
    high = x.astype(jnp.bfloat16)
    rest = x - high.astype(jnp.float32)
    middle = rest.astype(jnp.bfloat16)
    low = (rest - middle.astype(jnp.float32)).astype(jnp.bfloat16)
    return [high, middle, low]


def encode_body(dosages, observed, first, second, sums, held_d, held_o, sems):
    steps = sems.shape[1]
    samples, width = held_d.shape
    rows = samples // steps
    spans = [pl.ds(i * rows, rows) for i in range(steps)]
    copies = [
        [
            pltpu.make_async_copy(src.at[span], dst.at[span], sems.at[j, i])
            for j, (src, dst) in enumerate(((dosages, held_d), (observed, held_o)))
        ]
        for i, span in enumerate(spans)
    ]
    for pair in copies:
        for copy in pair:
            copy.start()
    parts = [jnp.zeros((8, width), jnp.int32)] * 3
    for span, pair in zip(spans, copies):
        for copy in pair:
            copy.wait()
        weights = held_o[span]
        known = held_d[span] * weights
        code = (known + (weights - 1)).astype(jnp.float32).astype(jnp.bfloat16)
        first[span] = code[:, :first.shape[1]]
        second[span] = code[:, first.shape[1]:]
        for i, part in enumerate((weights, known, known * known)):
            parts[i] += jnp.sum(part.reshape(rows // 8, 8, width), axis=0)
    rows_out = [jnp.sum(p, axis=0, keepdims=True) for p in parts]
    sums[...] = jnp.concatenate(rows_out + [jnp.zeros((5, width), jnp.int32)], axis=0)


def call(body, name, shapes, inputs, mib=32, in_hbm=False, scratch=(), events=()):
    place = pltpu.HBM if in_hbm else pltpu.VMEM
    n = len(inputs)
    skip = len(events)

    def with_events(*refs):
        body(*refs[:n], *refs[n + skip:])

    return pl.pallas_call(
        with_events,
        in_specs=[pl.BlockSpec(memory_space=place)] * n
        + [pl.BlockSpec(memory_space=pl.ANY)] * skip,
        out_specs=[pl.BlockSpec(memory_space=pltpu.VMEM)] * len(shapes),
        out_shape=[jax.ShapeDtypeStruct(shape, kind) for shape, kind in shapes],
        scratch_shapes=scratch,
        compiler_params=params(mib),
        cost_estimate=pl.CostEstimate(flops=0, bytes_accessed=0, transcendentals=0),
        name=name,
    )(*inputs, *events)


def encode(dosages, observed):
    samples, width = dosages.shape
    steps = 8
    cut = width // 2
    return call(
        encode_body,
        "encode",
        [
            ((samples, cut), jnp.bfloat16),
            ((samples, width - cut), jnp.bfloat16),
            ((8, width), jnp.int32),
        ],
        [dosages, observed],
        in_hbm=True,
        scratch=[
            pltpu.VMEM((samples, width), jnp.int32),
            pltpu.VMEM((samples, width), jnp.int32),
            pltpu.SemaphoreType.DMA((2, steps)),
        ],
    )


def variant_stats(sums):
    counts = jnp.maximum(sums[0], 1)
    n = counts.astype(jnp.float32)
    pivot = jnp.floor(sums[1].astype(jnp.float32) / n + 0.5).astype(jnp.int32)
    rest = (sums[1] - pivot * counts).astype(jnp.float32)
    squares = (sums[2] - 2 * pivot * sums[1] + pivot * pivot * sums[0]).astype(jnp.float32)
    spreads = (squares - rest * rest / n) / n * 1e-4
    means = pivot.astype(jnp.float32) + rest / n
    return means, lax.rsqrt(spreads + 1e-05) * 0.01


def standardize(code, means, scales):
    value = code.astype(jnp.float32)
    return jnp.where(value >= 0, (value - means) * scales, 0.0).astype(jnp.bfloat16)


def finish_body(first, second, *refs):
    sums_refs, (own, message) = refs[:-2], refs[-2:]
    samples, cut = first.shape
    sums = [sum(r[i:i + 1] for r in sums_refs) for i in range(3)]
    means, scales = variant_stats(sums)
    own[:, :cut] = standardize(first[...], means[:, :cut], scales[:, :cut])
    rest = standardize(second[...], means[:, cut:], scales[:, cut:])
    own[:, cut:] = rest
    message[:samples] = rest
    rows = split3(means[:, :cut]) + split3(scales[:, :cut])
    rows.append(jnp.zeros((TAIL - len(rows), cut), jnp.bfloat16))
    message[samples:] = jnp.concatenate(rows, axis=0)


def finish(first, second, all_sums, events):
    samples, cut = first.shape
    return call(
        finish_body,
        "finish",
        [((samples, 2 * cut), jnp.bfloat16), ((samples + TAIL, cut), jnp.bfloat16)],
        [first, second, *all_sums],
        events=events,
    )


def interleave_body(first, second, third_a, third_b, fourth, out):
    tile, width = first.shape
    count = min(tile, 64)
    size = BAND * count
    to_row = lax.broadcasted_iota(jnp.int32, (size, size), 0)
    from_row = lax.broadcasted_iota(jnp.int32, (size, size), 1)
    panel = sum((from_row >= k * count).astype(jnp.int32) for k in range(1, BAND))
    order = (to_row == (from_row - panel * count) * BAND + panel).astype(jnp.float32)
    order = order.astype(jnp.bfloat16)
    for i in range(tile // count):
        span = slice(i * count, (i + 1) * count)
        third = jnp.concatenate([third_a[span], third_b[span]], axis=1)
        rows = jnp.concatenate([first[span], second[span], third, fourth[span]], axis=0)
        turned = jnp.dot(order, rows, preferred_element_type=jnp.float32)
        out[span] = turned.astype(jnp.bfloat16).reshape(count, BAND, width)


def interleave(panels):
    rows, width = panels[0].shape
    tile = min(rows, 256)
    return pl.pallas_call(
        interleave_body,
        grid=(rows // tile,),
        in_specs=[pl.BlockSpec((tile, p.shape[1]), lambda i: (i, 0)) for p in panels],
        out_specs=pl.BlockSpec((tile, BAND, width), lambda i: (i, 0, 0)),
        out_shape=jax.ShapeDtypeStruct((rows, BAND, width), jnp.bfloat16),
        compiler_params=params(32),
        name="interleave",
    )(*panels)


def product(whole, cols, distance):
    n_smp = lax.axis_size("smp")
    owned = whole.shape[1] // n_smp
    place = lax.rem(lax.axis_index("smp") + distance, n_smp)
    left = whole[:, pl.ds(pl.multiple_of(place * owned, owned), owned)]
    out = lax.dot_general(left, cols, (((0,), (0,)), ((), ())), preferred_element_type=jnp.float32)
    return out * (1.0 / (whole.shape[0] * n_smp))


def send_parts(whole, cols, parts):
    for d, ref in enumerate(parts):
        ref[...] = product(whole, cols, d + 1).astype(jnp.bfloat16)


def gather_body(n_sub, n_held, *refs):
    held, cols, whole, parts = refs[:n_held], refs[n_held], refs[n_held + 1], refs[n_held + 2:]
    width = held[0].shape[1]
    pieces = (n_held - 1) // (n_sub - 1)
    count = whole.shape[0] // pieces
    me = lax.axis_index("sub")

    def span(d):
        place = lax.rem(me - d + n_sub, n_sub)
        return pl.ds(pl.multiple_of(place * width, width), width)

    whole[:, span(0)] = held[0][...]
    for d in range(1, n_sub):
        for i in range(pieces):
            whole[i * count:(i + 1) * count, span(d)] = held[1 + (d - 1) * pieces + i][...]
    send_parts(whole, cols[...], parts)


def from_tail(tail):
    rows = [tail[i:i + 1].astype(jnp.float32) for i in range(6)]
    return (rows[0] + rows[1]) + rows[2], (rows[3] + rows[4]) + rows[5]


def assemble_body(first, message, out):
    samples, cut = first.shape
    out[:, :cut] = standardize(first[...], *from_tail(message[samples:]))
    out[:, cut:] = message[:samples]


def near_body(whole, first, message, cols, half, *parts):
    assemble_body(first, message, cols)
    half[...] = cols[:, :half.shape[1]]
    send_parts(whole, cols[...], parts)


def far_body(whole, cols, *parts):
    send_parts(whole, cols[:whole.shape[0]], parts)


def total_body(whole, cols, *refs):
    *arrived, out = refs
    total = product(whole, cols[:whole.shape[0]], 0).astype(jnp.bfloat16).astype(jnp.float32)
    for ref in arrived:
        total = total + ref[...].astype(jnp.float32)
    out[...] = total.astype(jnp.bfloat16)


def fence_body(*refs):
    refs[-1][...] = jnp.zeros_like(refs[-1])


def fence(weight, *events):
    return pl.pallas_call(
        fence_body,
        in_specs=[pl.BlockSpec(memory_space=pl.ANY)] * len(events),
        out_specs=pl.BlockSpec(memory_space=pltpu.VMEM),
        out_shape=jax.ShapeDtypeStruct((8, 128), jnp.float32),
        compiler_params=params(1),
        cost_estimate=pl.CostEstimate(flops=weight * 10**9, bytes_accessed=0, transcendentals=0),
        name="fence",
    )(*events)


def together(*arrays):
    return lax.optimization_barrier(arrays)


def on_device(dosages, observed):
    n_var = lax.axis_size("var")
    n_smp = lax.axis_size("smp")
    n_sub = lax.axis_size("sub")
    samples, width = dosages.shape
    rows_owned = width * n_sub // n_smp

    def along(x, distance, keep):
        route = [
            (i, i + distance) for i in range(n_var) if 0 <= i + distance < n_var and keep(i)
        ]
        return lax.ppermute(x, "var", route)

    def down(x):
        return along(x, -1, lambda i: True)

    def down_again(x):
        return along(x, -1, lambda i: i + 1 < n_var)

    def up_two(x):
        return along(x, 2, lambda i: i + 3 < n_var)

    def holds_three(i):
        return i >= 2 and i + 1 < n_var

    def down_two(x):
        return along(x, -2, holds_three)

    def swapped(x, axis, distance, keep=None):
        n = lax.axis_size(axis)
        if keep is None:
            return lax.ppermute(x, axis, [(i, (i + distance) % n) for i in range(n)])
        route = [
            (v * n + i, v * n + (i + distance) % n)
            for v in range(n_var)
            if keep(v)
            for i in range(n)
        ]
        return lax.ppermute(x, ("var", axis), route)

    def others_of(part, pieces):
        count = part.shape[0] // pieces
        cuts = [part[i * count:(i + 1) * count] for i in range(pieces)]
        return [swapped(c, "sub", d) for d in range(1, n_sub) for c in cuts]

    def sent(parts, keep=None):
        return [swapped(p, "smp", d + 1, keep) for d, p in enumerate(parts)]

    def part_shapes(columns):
        return [((rows_owned, columns), jnp.bfloat16)] * (n_smp - 1)

    def gather(part, others, cols, name, events):
        block = ((samples, width * n_sub), jnp.bfloat16)
        body = functools.partial(gather_body, n_sub, 1 + len(others))
        shapes = [block] + part_shapes(width)
        whole, *parts = call(body, name, shapes, [part, *others, cols], events=events)
        return whole, parts

    def total(whole, cols, arrived, name, events):
        shape = ((rows_owned, cols.shape[1]), jnp.bfloat16)
        return call(total_body, name, [shape], [whole, cols, *arrived], events=events)[0]

    first, second, sums_own = encode(dosages, observed)
    near_a = down(first)
    step = fence(20, first)
    sums_own, first_up, step = together(sums_own, first, step)
    up_a = up_two(first_up)
    arrived_sums = [swapped(sums_own, "smp", d) for d in range(1, n_smp)]
    step = fence(20, step)
    own, message = finish(first, second, [sums_own] + arrived_sums, [step])
    near_b, up_b = down(message), up_two(message)
    others = others_of(own, 1)
    step = fence(20, own)

    whole, part0 = gather(own, others, own, "gather0", [near_a, step])
    got0 = sent(part0)
    near_b, whole = together(near_b, whole)
    far_b = down_again(near_b)
    half = ((samples, width // 2), jnp.bfloat16)
    cols1, near_a, *part1 = call(
        near_body,
        "near",
        [((samples, width), jnp.bfloat16), half] + part_shapes(width),
        [whole, near_a, near_b],
    )
    far_a = down_again(near_a)
    (rows3,) = call(
        assemble_body,
        "rows3",
        [((samples, width), jnp.bfloat16)],
        [up_a, up_b],
        events=[cols1],
    )
    others3 = others_of(rows3, 2)
    panel0 = total(whole, own, got0, "total0", [rows3])
    whole3, part3 = gather(rows3, others3, cols1, "gather3", [fence(3, panel0)])
    got3 = sent(part3, holds_three)
    part2_b = call(far_body, "far_b", part_shapes(width // 2), [whole, far_b], events=[whole3])
    got2_b = sent(part2_b)
    step = fence(12, *part2_b)
    panel3 = total(whole3, cols1, got3, "total3", [step])
    *part1, panel3 = together(*part1, panel3)
    got1 = sent(part1)
    panel3 = down_two(panel3)
    part2_a = call(
        far_body, "far_a", part_shapes(width // 2), [whole, far_a], events=[*part1]
    )
    got2_a = sent(part2_a, lambda v: v + 2 < n_var)
    panel2_b = total(whole, far_b, got2_b, "total2b", [*part2_a])
    step = fence(3, panel2_b)
    panel1 = total(whole, cols1, got1, "total1", [step])
    panel2_a = total(whole, far_a, got2_a, "total2a", [panel1])
    return interleave([panel0, panel1, panel2_a, panel2_b, panel3])


def solution(mesh):
    in_specs = (P("smp", ("grp", "var", "sub")), P("smp", ("grp", "var", "sub")))
    out_specs = P(("grp", "var", "smp"), None, "sub")
    return jax.shard_map(
        on_device, mesh=mesh, in_specs=in_specs, out_specs=out_specs, check_vma=False
    )
```

```python
import functools

import jax
import jax.numpy as jnp
from jax import lax
from jax.experimental import pallas as pl
from jax.experimental.pallas import tpu as pltpu
from jax.sharding import PartitionSpec as P

BAND = 4
TAIL = 16


def params(mib):
    return pltpu.CompilerParams(vmem_limit_bytes=mib * 1024 * 1024)


def split3(x):
    high = x.astype(jnp.bfloat16)
    rest = x - high.astype(jnp.float32)
    middle = rest.astype(jnp.bfloat16)
    low = (rest - middle.astype(jnp.float32)).astype(jnp.bfloat16)
    return [high, middle, low]


def encode_body(dosages, observed, first, second, sums, held_d, held_o, sems):
    steps = sems.shape[1]
    samples, width = held_d.shape
    rows = samples // steps
    spans = [pl.ds(i * rows, rows) for i in range(steps)]
    copies = [
        [
            pltpu.make_async_copy(src.at[span], dst.at[span], sems.at[j, i])
            for j, (src, dst) in enumerate(((dosages, held_d), (observed, held_o)))
        ]
        for i, span in enumerate(spans)
    ]
    for pair in copies:
        for copy in pair:
            copy.start()
    parts = [jnp.zeros((8, width), jnp.int32)] * 3
    for span, pair in zip(spans, copies):
        for copy in pair:
            copy.wait()
        weights = held_o[span]
        known = held_d[span] * weights
        code = (known + (weights - 1)).astype(jnp.float32).astype(jnp.bfloat16)
        first[span] = code[:, :first.shape[1]]
        second[span] = code[:, first.shape[1]:]
        for i, part in enumerate((weights, known, known * known)):
            parts[i] += jnp.sum(part.reshape(rows // 8, 8, width), axis=0)
    rows_out = [jnp.sum(p, axis=0, keepdims=True) for p in parts]
    sums[...] = jnp.concatenate(rows_out + [jnp.zeros((5, width), jnp.int32)], axis=0)


def call(body, name, shapes, inputs, mib=32, in_hbm=False, scratch=(), events=()):
    place = pltpu.HBM if in_hbm else pltpu.VMEM
    n = len(inputs)
    skip = len(events)

    def with_events(*refs):
        body(*refs[:n], *refs[n + skip:])

    return pl.pallas_call(
        with_events,
        in_specs=[pl.BlockSpec(memory_space=place)] * n
        + [pl.BlockSpec(memory_space=pl.ANY)] * skip,
        out_specs=[pl.BlockSpec(memory_space=pltpu.VMEM)] * len(shapes),
        out_shape=[jax.ShapeDtypeStruct(shape, kind) for shape, kind in shapes],
        scratch_shapes=scratch,
        compiler_params=params(mib),
        cost_estimate=pl.CostEstimate(flops=0, bytes_accessed=0, transcendentals=0),
        name=name,
    )(*inputs, *events)


def encode(dosages, observed):
    samples, width = dosages.shape
    steps = 8
    cut = width // 2
    return call(
        encode_body,
        "encode",
        [
            ((samples, cut), jnp.bfloat16),
            ((samples, width - cut), jnp.bfloat16),
            ((8, width), jnp.int32),
        ],
        [dosages, observed],
        in_hbm=True,
        scratch=[
            pltpu.VMEM((samples, width), jnp.int32),
            pltpu.VMEM((samples, width), jnp.int32),
            pltpu.SemaphoreType.DMA((2, steps)),
        ],
    )


def variant_stats(sums):
    counts = jnp.maximum(sums[0], 1)
    n = counts.astype(jnp.float32)
    pivot = jnp.floor(sums[1].astype(jnp.float32) / n + 0.5).astype(jnp.int32)
    rest = (sums[1] - pivot * counts).astype(jnp.float32)
    squares = (sums[2] - 2 * pivot * sums[1] + pivot * pivot * sums[0]).astype(jnp.float32)
    spreads = (squares - rest * rest / n) / n * 1e-4
    means = pivot.astype(jnp.float32) + rest / n
    return means, lax.rsqrt(spreads + 1e-05) * 0.01


def standardize(code, means, scales):
    value = code.astype(jnp.float32)
    return jnp.where(value >= 0, (value - means) * scales, 0.0).astype(jnp.bfloat16)


def finish_body(first, second, *refs):
    sums_refs, (own, message) = refs[:-2], refs[-2:]
    samples, cut = first.shape
    sums = [sum(r[i:i + 1] for r in sums_refs) for i in range(3)]
    means, scales = variant_stats(sums)
    own[:, :cut] = standardize(first[...], means[:, :cut], scales[:, :cut])
    rest = standardize(second[...], means[:, cut:], scales[:, cut:])
    own[:, cut:] = rest
    message[:samples] = rest
    rows = split3(means[:, :cut]) + split3(scales[:, :cut])
    rows.append(jnp.zeros((TAIL - len(rows), cut), jnp.bfloat16))
    message[samples:] = jnp.concatenate(rows, axis=0)


def finish(first, second, all_sums, events):
    samples, cut = first.shape
    return call(
        finish_body,
        "finish",
        [((samples, 2 * cut), jnp.bfloat16), ((samples + TAIL, cut), jnp.bfloat16)],
        [first, second, *all_sums],
        events=events,
    )


def interleave_body(first, second, third_a, third_b, fourth, out):
    tile, width = first.shape
    count = min(tile, 64)
    size = BAND * count
    to_row = lax.broadcasted_iota(jnp.int32, (size, size), 0)
    from_row = lax.broadcasted_iota(jnp.int32, (size, size), 1)
    panel = sum((from_row >= k * count).astype(jnp.int32) for k in range(1, BAND))
    order = (to_row == (from_row - panel * count) * BAND + panel).astype(jnp.float32)
    order = order.astype(jnp.bfloat16)
    for i in range(tile // count):
        span = slice(i * count, (i + 1) * count)
        third = jnp.concatenate([third_a[span], third_b[span]], axis=1)
        rows = jnp.concatenate([first[span], second[span], third, fourth[span]], axis=0)
        turned = jnp.dot(order, rows, preferred_element_type=jnp.float32)
        out[span] = turned.astype(jnp.bfloat16).reshape(count, BAND, width)


def interleave(panels):
    rows, width = panels[0].shape
    tile = min(rows, 256)
    return pl.pallas_call(
        interleave_body,
        grid=(rows // tile,),
        in_specs=[pl.BlockSpec((tile, p.shape[1]), lambda i: (i, 0)) for p in panels],
        out_specs=pl.BlockSpec((tile, BAND, width), lambda i: (i, 0, 0)),
        out_shape=jax.ShapeDtypeStruct((rows, BAND, width), jnp.bfloat16),
        compiler_params=params(32),
        name="interleave",
    )(*panels)


def product(whole, cols, distance):
    n_smp = lax.axis_size("smp")
    owned = whole.shape[1] // n_smp
    place = lax.rem(lax.axis_index("smp") + distance, n_smp)
    left = whole[:, pl.ds(pl.multiple_of(place * owned, owned), owned)]
    out = lax.dot_general(left, cols, (((0,), (0,)), ((), ())), preferred_element_type=jnp.float32)
    return out * (1.0 / (whole.shape[0] * n_smp))


def send_parts(whole, cols, parts):
    for d, ref in enumerate(parts):
        ref[...] = product(whole, cols, d + 1).astype(jnp.bfloat16)


def holds_three():
    place = lax.axis_index("var")
    return jnp.logical_and(place >= 2, place + 1 < lax.axis_size("var"))


def choose(condition, when_true, when_false):
    pl.when(condition)(when_true)
    pl.when(jnp.logical_not(condition))(when_false)


def copy_parts(spare, parts):
    for source, ref in zip(spare, parts):
        ref[...] = source[...]


def gather_body(n_sub, n_held, n_spare, *refs):
    held, (cols, *rest) = refs[:n_held], refs[n_held:]
    spare, whole, parts = rest[:n_spare], rest[n_spare], rest[n_spare + 1:]
    width = held[0].shape[1]
    pieces = (n_held - 1) // (n_sub - 1)
    count = whole.shape[0] // pieces
    me = lax.axis_index("sub")

    def span(d):
        place = lax.rem(me - d + n_sub, n_sub)
        return pl.ds(pl.multiple_of(place * width, width), width)

    whole[:, span(0)] = held[0][...]
    for d in range(1, n_sub):
        for i in range(pieces):
            whole[i * count:(i + 1) * count, span(d)] = held[1 + (d - 1) * pieces + i][...]
    if not spare:
        send_parts(whole, cols[...], parts)
        return
    choose(
        holds_three(),
        lambda: send_parts(whole, cols[...], parts),
        lambda: copy_parts(spare, parts),
    )


def from_tail(tail):
    rows = [tail[i:i + 1].astype(jnp.float32) for i in range(6)]
    return (rows[0] + rows[1]) + rows[2], (rows[3] + rows[4]) + rows[5]


def assemble_body(first, message, out):
    samples, cut = first.shape
    out[:, :cut] = standardize(first[...], *from_tail(message[samples:]))
    out[:, cut:] = message[:samples]


def near_body(whole, first, message, cols, half, *parts):
    assemble_body(first, message, cols)
    half[...] = cols[:, :half.shape[1]]
    send_parts(whole, cols[...], parts)


def far_body(begin, n_spare, whole, cols, *refs):
    spare, parts = refs[:n_spare], refs[n_spare:]

    def own():
        send_parts(whole, cols[:whole.shape[0]], parts)

    if not spare:
        own()
        return
    span = slice(begin, begin + cols.shape[1])
    choose(holds_three(), lambda: copy_parts([r.at[:, span] for r in spare], parts), own)


def summed(whole, cols, arrived):
    total = product(whole, cols, 0).astype(jnp.bfloat16).astype(jnp.float32)
    for part in arrived:
        total = total + part.astype(jnp.float32)
    return total.astype(jnp.bfloat16)


def total_body(whole, cols, *refs):
    *arrived, out = refs
    out[...] = summed(whole, cols[:whole.shape[0]], [r[...] for r in arrived])


def total_or_none_body(whole, cols, *refs):
    out = refs[-1]

    def none():
        out[...] = jnp.zeros_like(out)

    choose(holds_three(), none, lambda: total_body(whole, cols, *refs))


def total_near_body(n_parts, whole, cols, *refs):
    first, later, out = refs[:n_parts], refs[n_parts:-1], refs[-1]

    def displaced():
        begin = 0
        for i in range(0, len(later), n_parts):
            group = later[i:i + n_parts]
            span = slice(begin, begin + group[0].shape[1])
            out[:, span] = summed(whole, cols[:, span], [r[...] for r in group])
            begin = span.stop

    choose(holds_three(), displaced, lambda: total_body(whole, cols, *first, out))


def fence_body(*refs):
    refs[-1][...] = jnp.zeros_like(refs[-1])


def fence(weight, *events):
    return pl.pallas_call(
        fence_body,
        in_specs=[pl.BlockSpec(memory_space=pl.ANY)] * len(events),
        out_specs=pl.BlockSpec(memory_space=pltpu.VMEM),
        out_shape=jax.ShapeDtypeStruct((8, 128), jnp.float32),
        compiler_params=params(1),
        cost_estimate=pl.CostEstimate(flops=weight * 10**9, bytes_accessed=0, transcendentals=0),
        name="fence",
    )(*events)


def together(*arrays):
    return lax.optimization_barrier(arrays)


def on_device(dosages, observed):
    n_var = lax.axis_size("var")
    n_smp = lax.axis_size("smp")
    n_sub = lax.axis_size("sub")
    samples, width = dosages.shape
    rows_owned = width * n_sub // n_smp

    def along(x, distance, keep):
        route = [
            (i, i + distance) for i in range(n_var) if 0 <= i + distance < n_var and keep(i)
        ]
        return lax.ppermute(x, "var", route)

    def down(x):
        return along(x, -1, lambda i: True)

    def down_again(x):
        return along(x, -1, lambda i: i + 1 < n_var)

    def up_two(x):
        return along(x, 2, lambda i: i + 3 < n_var)

    def holds(i):
        return i >= 2 and i + 1 < n_var

    shared = not any(holds(i) and i + 2 < n_var for i in range(n_var))

    def down_two(x):
        return along(x, -2, holds)

    def swapped(x, axis, distance, keep=None):
        n = lax.axis_size(axis)
        if keep is None:
            return lax.ppermute(x, axis, [(i, (i + distance) % n) for i in range(n)])
        route = [
            (v * n + i, v * n + (i + distance) % n)
            for v in range(n_var)
            if keep(v)
            for i in range(n)
        ]
        return lax.ppermute(x, ("var", axis), route)

    def others_of(part, pieces):
        count = part.shape[0] // pieces
        cuts = [part[i * count:(i + 1) * count] for i in range(pieces)]
        return [swapped(c, "sub", d) for d in range(1, n_sub) for c in cuts]

    def sent(parts, keep=None):
        return [swapped(p, "smp", d + 1, keep) for d, p in enumerate(parts)]

    def part_shapes(columns):
        return [((rows_owned, columns), jnp.bfloat16)] * (n_smp - 1)

    def gather(part, others, cols, name, events, spare=()):
        block = ((samples, width * n_sub), jnp.bfloat16)
        body = functools.partial(gather_body, n_sub, 1 + len(others), len(spare))
        shapes = [block] + part_shapes(width)
        inputs = [part, *others, cols, *spare]
        whole, *parts = call(body, name, shapes, inputs, events=events)
        return whole, parts

    def far_parts(cols, begin, name, events):
        spare = part1 if shared else []
        body = functools.partial(far_body, begin, len(spare))
        return call(body, name, part_shapes(width // 2), [whole, cols, *spare], events=events)

    def total(whole, cols, arrived, name, events, body=total_body):
        shape = ((rows_owned, cols.shape[1]), jnp.bfloat16)
        return call(body, name, [shape], [whole, cols, *arrived], events=events)[0]

    first, second, sums_own = encode(dosages, observed)
    near_a = down(first)
    step = fence(20, first)
    sums_own, first_up, step = together(sums_own, first, step)
    up_a = up_two(first_up)
    arrived_sums = [swapped(sums_own, "smp", d) for d in range(1, n_smp)]
    step = fence(20, step)
    own, message = finish(first, second, [sums_own] + arrived_sums, [step])
    near_b, up_b = down(message), up_two(message)
    others = others_of(own, 1)
    step = fence(20, own)

    whole, part0 = gather(own, others, own, "gather0", [near_a, step])
    got0 = sent(part0)
    near_b, whole = together(near_b, whole)
    far_b = down_again(near_b)
    half = ((samples, width // 2), jnp.bfloat16)
    cols1, near_a, *part1 = call(
        near_body,
        "near",
        [((samples, width), jnp.bfloat16), half] + part_shapes(width),
        [whole, near_a, near_b],
    )
    far_a = down_again(near_a)
    (rows3,) = call(
        assemble_body,
        "rows3",
        [((samples, width), jnp.bfloat16)],
        [up_a, up_b],
        events=[cols1],
    )
    others3 = others_of(rows3, 2)
    panel0 = total(whole, own, got0, "total0", [rows3])
    whole3, part3 = gather(rows3, others3, cols1, "gather3", [fence(3, panel0)], part1)
    got3 = sent(part3)
    part2_b = far_parts(far_b, width // 2, "far_b", [whole3])
    got2_b = sent(part2_b)
    panel3 = total(whole3, cols1, got3, "total3", [fence(12, *part2_b)])
    later = []
    if not shared:
        *part1, panel3 = together(*part1, panel3)
        later = sent(part1, holds)
    part2_a = far_parts(far_a, 0, "far_a", [panel3])
    panel3 = down_two(panel3)
    got2_a = sent(part2_a)
    if shared:
        later = got2_a + got2_b
    ending = total_or_none_body if shared else total_body
    panel2_b = total(whole, far_b, got2_b, "total2b", [*part2_a], ending)
    panel1 = total(
        whole,
        cols1,
        got3 + later,
        "total1",
        [fence(3, panel2_b)],
        functools.partial(total_near_body, n_smp - 1),
    )
    panel2_a = total(whole, far_a, got2_a, "total2a", [panel1], ending)
    return interleave([panel0, panel1, panel2_a, panel2_b, panel3])


def solution(mesh):
    in_specs = (P("smp", ("grp", "var", "sub")), P("smp", ("grp", "var", "sub")))
    out_specs = P(("grp", "var", "smp"), None, "sub")
    return jax.shard_map(
        on_device, mesh=mesh, in_specs=in_specs, out_specs=out_specs, check_vma=False
    )
```

```python
import functools

import jax
import jax.numpy as jnp
from jax import lax
from jax.experimental import pallas as pl
from jax.experimental.pallas import tpu as pltpu
from jax.sharding import PartitionSpec as P

BAND = 4
TAIL = 16


def params(mib):
    return pltpu.CompilerParams(vmem_limit_bytes=mib * 1024 * 1024)


def split3(x):
    high = x.astype(jnp.bfloat16)
    rest = x - high.astype(jnp.float32)
    middle = rest.astype(jnp.bfloat16)
    low = (rest - middle.astype(jnp.float32)).astype(jnp.bfloat16)
    return [high, middle, low]


def encode_body(dosages, observed, first, second, sums, held_d, held_o, sems):
    steps = sems.shape[1]
    samples, width = held_d.shape
    rows = samples // steps
    spans = [pl.ds(i * rows, rows) for i in range(steps)]
    copies = [
        [
            pltpu.make_async_copy(src.at[span], dst.at[span], sems.at[j, i])
            for j, (src, dst) in enumerate(((dosages, held_d), (observed, held_o)))
        ]
        for i, span in enumerate(spans)
    ]
    for pair in copies:
        for copy in pair:
            copy.start()
    parts = [jnp.zeros((8, width), jnp.int32)] * 3
    for span, pair in zip(spans, copies):
        for copy in pair:
            copy.wait()
        weights = held_o[span]
        known = held_d[span] * weights
        code = (known + (weights - 1)).astype(jnp.float32).astype(jnp.bfloat16)
        first[span] = code[:, :first.shape[1]]
        second[span] = code[:, first.shape[1]:]
        for i, part in enumerate((weights, known, known * known)):
            parts[i] += jnp.sum(part.reshape(rows // 8, 8, width), axis=0)
    rows_out = [jnp.sum(p, axis=0, keepdims=True) for p in parts]
    sums[...] = jnp.concatenate(rows_out + [jnp.zeros((5, width), jnp.int32)], axis=0)


def call(body, name, shapes, inputs, mib=32, in_hbm=False, scratch=(), events=()):
    place = pltpu.HBM if in_hbm else pltpu.VMEM
    n = len(inputs)
    skip = len(events)

    def with_events(*refs):
        body(*refs[:n], *refs[n + skip:])

    return pl.pallas_call(
        with_events,
        in_specs=[pl.BlockSpec(memory_space=place)] * n
        + [pl.BlockSpec(memory_space=pl.ANY)] * skip,
        out_specs=[pl.BlockSpec(memory_space=pltpu.VMEM)] * len(shapes),
        out_shape=[jax.ShapeDtypeStruct(shape, kind) for shape, kind in shapes],
        scratch_shapes=scratch,
        compiler_params=params(mib),
        cost_estimate=pl.CostEstimate(flops=0, bytes_accessed=0, transcendentals=0),
        name=name,
    )(*inputs, *events)


def encode(dosages, observed):
    samples, width = dosages.shape
    steps = 8
    cut = width // 2
    return call(
        encode_body,
        "encode",
        [
            ((samples, cut), jnp.bfloat16),
            ((samples, width - cut), jnp.bfloat16),
            ((8, width), jnp.int32),
        ],
        [dosages, observed],
        mib=52,
        in_hbm=True,
        scratch=[
            pltpu.VMEM((samples, width), jnp.int32),
            pltpu.VMEM((samples, width), jnp.int32),
            pltpu.SemaphoreType.DMA((2, steps)),
        ],
    )


def variant_stats(sums):
    counts = jnp.maximum(sums[0], 1)
    n = counts.astype(jnp.float32)
    pivot = jnp.floor(sums[1].astype(jnp.float32) / n + 0.5).astype(jnp.int32)
    rest = (sums[1] - pivot * counts).astype(jnp.float32)
    squares = (sums[2] - 2 * pivot * sums[1] + pivot * pivot * sums[0]).astype(jnp.float32)
    spreads = (squares - rest * rest / n) / n * 1e-4
    means = pivot.astype(jnp.float32) + rest / n
    return means, lax.rsqrt(spreads + 1e-05) * 0.01


def standardize(code, means, scales):
    value = code.astype(jnp.float32)
    return jnp.where(value >= 0, (value - means) * scales, 0.0).astype(jnp.bfloat16)


def finish_body(first, second, *refs):
    sums_refs, (own, message) = refs[:-2], refs[-2:]
    samples, cut = first.shape
    sums = [sum(r[i:i + 1] for r in sums_refs) for i in range(3)]
    means, scales = variant_stats(sums)
    own[:, :cut] = standardize(first[...], means[:, :cut], scales[:, :cut])
    rest = standardize(second[...], means[:, cut:], scales[:, cut:])
    own[:, cut:] = rest
    message[:samples] = rest
    rows = split3(means[:, :cut]) + split3(scales[:, :cut])
    rows.append(jnp.zeros((TAIL - len(rows), cut), jnp.bfloat16))
    message[samples:] = jnp.concatenate(rows, axis=0)


def finish(first, second, all_sums, events):
    samples, cut = first.shape
    return call(
        finish_body,
        "finish",
        [((samples, 2 * cut), jnp.bfloat16), ((samples + TAIL, cut), jnp.bfloat16)],
        [first, second, *all_sums],
        events=events,
    )


def interleave_body(first, second, third_a, third_b, fourth, out):
    tile, width = first.shape
    count = min(tile, 64)
    size = BAND * count
    to_row = lax.broadcasted_iota(jnp.int32, (size, size), 0)
    from_row = lax.broadcasted_iota(jnp.int32, (size, size), 1)
    panel = sum((from_row >= k * count).astype(jnp.int32) for k in range(1, BAND))
    order = (to_row == (from_row - panel * count) * BAND + panel).astype(jnp.float32)
    order = order.astype(jnp.bfloat16)
    for i in range(tile // count):
        span = slice(i * count, (i + 1) * count)
        third = jnp.concatenate([third_a[span], third_b[span]], axis=1)
        rows = jnp.concatenate([first[span], second[span], third, fourth[span]], axis=0)
        turned = jnp.dot(order, rows, preferred_element_type=jnp.float32)
        out[span] = turned.astype(jnp.bfloat16).reshape(count, BAND, width)


def interleave(panels):
    rows, width = panels[0].shape
    tile = min(rows, 256)
    return pl.pallas_call(
        interleave_body,
        grid=(rows // tile,),
        in_specs=[pl.BlockSpec((tile, p.shape[1]), lambda i: (i, 0)) for p in panels],
        out_specs=pl.BlockSpec((tile, BAND, width), lambda i: (i, 0, 0)),
        out_shape=jax.ShapeDtypeStruct((rows, BAND, width), jnp.bfloat16),
        compiler_params=params(32),
        name="interleave",
    )(*panels)


def product(whole, cols, distance):
    n_smp = lax.axis_size("smp")
    owned = whole.shape[1] // n_smp
    place = lax.rem(lax.axis_index("smp") + distance, n_smp)
    left = whole[:, pl.ds(pl.multiple_of(place * owned, owned), owned)]
    out = lax.dot_general(left, cols, (((0,), (0,)), ((), ())), preferred_element_type=jnp.float32)
    return out * (1.0 / (whole.shape[0] * n_smp))


def send_parts(whole, cols, parts):
    for d, ref in enumerate(parts):
        ref[...] = product(whole, cols, d + 1).astype(jnp.bfloat16)


def holds_three():
    place = lax.axis_index("var")
    return jnp.logical_and(place >= 2, place + 1 < lax.axis_size("var"))


def choose(condition, when_true, when_false):
    pl.when(condition)(when_true)
    pl.when(jnp.logical_not(condition))(when_false)


def copy_parts(spare, parts):
    for source, ref in zip(spare, parts):
        ref[...] = source[...]


def gather_body(n_sub, n_held, n_spare, *refs):
    held, (cols, *rest) = refs[:n_held], refs[n_held:]
    spare, whole, parts = rest[:n_spare], rest[n_spare], rest[n_spare + 1:]
    width = held[0].shape[1]
    pieces = (n_held - 1) // (n_sub - 1)
    count = whole.shape[0] // pieces
    me = lax.axis_index("sub")

    def span(d):
        place = lax.rem(me - d + n_sub, n_sub)
        return pl.ds(pl.multiple_of(place * width, width), width)

    whole[:, span(0)] = held[0][...]
    for d in range(1, n_sub):
        for i in range(pieces):
            whole[i * count:(i + 1) * count, span(d)] = held[1 + (d - 1) * pieces + i][...]
    if not spare:
        send_parts(whole, cols[...], parts)
        return
    choose(
        holds_three(),
        lambda: send_parts(whole, cols[...], parts),
        lambda: copy_parts(spare, parts),
    )


def from_tail(tail):
    rows = [tail[i:i + 1].astype(jnp.float32) for i in range(6)]
    return (rows[0] + rows[1]) + rows[2], (rows[3] + rows[4]) + rows[5]


def assemble_body(first, message, out):
    samples, cut = first.shape
    out[:, :cut] = standardize(first[...], *from_tail(message[samples:]))
    out[:, cut:] = message[:samples]


def near_body(whole, first, message, cols, half, *parts):
    assemble_body(first, message, cols)
    half[...] = cols[:, :half.shape[1]]
    send_parts(whole, cols[...], parts)


def far_body(begin, n_spare, whole, cols, *refs):
    spare, parts = refs[:n_spare], refs[n_spare:]

    def own():
        send_parts(whole, cols[:whole.shape[0]], parts)

    if not spare:
        own()
        return
    span = slice(begin, begin + cols.shape[1])
    choose(holds_three(), lambda: copy_parts([r.at[:, span] for r in spare], parts), own)


def summed(whole, cols, arrived):
    total = product(whole, cols, 0).astype(jnp.bfloat16).astype(jnp.float32)
    for part in arrived:
        total = total + part.astype(jnp.float32)
    return total.astype(jnp.bfloat16)


def total_body(whole, cols, *refs):
    *arrived, out = refs
    out[...] = summed(whole, cols[:whole.shape[0]], [r[...] for r in arrived])


def total_or_none_body(whole, cols, *refs):
    out = refs[-1]

    def none():
        out[...] = jnp.zeros_like(out)

    choose(holds_three(), none, lambda: total_body(whole, cols, *refs))


def total_near_body(n_parts, whole, cols, *refs):
    first, later, out = refs[:n_parts], refs[n_parts:-1], refs[-1]

    def displaced():
        begin = 0
        for i in range(0, len(later), n_parts):
            group = later[i:i + n_parts]
            span = slice(begin, begin + group[0].shape[1])
            out[:, span] = summed(whole, cols[:, span], [r[...] for r in group])
            begin = span.stop

    choose(holds_three(), displaced, lambda: total_body(whole, cols, *first, out))


def fence_body(*refs):
    refs[-1][...] = jnp.zeros_like(refs[-1])


def fence(weight, *events):
    return pl.pallas_call(
        fence_body,
        in_specs=[pl.BlockSpec(memory_space=pl.ANY)] * len(events),
        out_specs=pl.BlockSpec(memory_space=pltpu.VMEM),
        out_shape=jax.ShapeDtypeStruct((8, 128), jnp.float32),
        compiler_params=params(1),
        cost_estimate=pl.CostEstimate(flops=weight * 10**9, bytes_accessed=0, transcendentals=0),
        name="fence",
    )(*events)


def together(*arrays):
    return lax.optimization_barrier(arrays)


def on_device(dosages, observed):
    n_var = lax.axis_size("var")
    n_smp = lax.axis_size("smp")
    n_sub = lax.axis_size("sub")
    samples, width = dosages.shape
    rows_owned = width * n_sub // n_smp

    def along(x, distance, keep):
        route = [
            (i, i + distance) for i in range(n_var) if 0 <= i + distance < n_var and keep(i)
        ]
        return lax.ppermute(x, "var", route)

    def down(x):
        return along(x, -1, lambda i: True)

    def down_again(x):
        return along(x, -1, lambda i: i + 1 < n_var)

    def up_two(x):
        return along(x, 2, lambda i: i + 3 < n_var)

    def holds(i):
        return i >= 2 and i + 1 < n_var

    shared = not any(holds(i) and i + 2 < n_var for i in range(n_var))

    def down_two(x):
        return along(x, -2, holds)

    def swapped(x, axis, distance, keep=None):
        n = lax.axis_size(axis)
        if keep is None:
            return lax.ppermute(x, axis, [(i, (i + distance) % n) for i in range(n)])
        route = [
            (v * n + i, v * n + (i + distance) % n)
            for v in range(n_var)
            if keep(v)
            for i in range(n)
        ]
        return lax.ppermute(x, ("var", axis), route)

    def others_of(part, pieces):
        count = part.shape[0] // pieces
        cuts = [part[i * count:(i + 1) * count] for i in range(pieces)]
        return [swapped(c, "sub", d) for d in range(1, n_sub) for c in cuts]

    def sent(parts, keep=None):
        return [swapped(p, "smp", d + 1, keep) for d, p in enumerate(parts)]

    def part_shapes(columns):
        return [((rows_owned, columns), jnp.bfloat16)] * (n_smp - 1)

    def gather(part, others, cols, name, events, spare=()):
        block = ((samples, width * n_sub), jnp.bfloat16)
        body = functools.partial(gather_body, n_sub, 1 + len(others), len(spare))
        shapes = [block] + part_shapes(width)
        inputs = [part, *others, cols, *spare]
        whole, *parts = call(body, name, shapes, inputs, events=events)
        return whole, parts

    def far_parts(cols, begin, name, events):
        spare = part1 if shared else []
        body = functools.partial(far_body, begin, len(spare))
        return call(body, name, part_shapes(width // 2), [whole, cols, *spare], events=events)

    def total(whole, cols, arrived, name, events, body=total_body):
        shape = ((rows_owned, cols.shape[1]), jnp.bfloat16)
        return call(body, name, [shape], [whole, cols, *arrived], events=events)[0]

    first, second, sums_own = encode(dosages, observed)
    near_a = down(first)
    step = fence(20, first)
    sums_own, first_up, step = together(sums_own, first, step)
    up_a = up_two(first_up)
    arrived_sums = [swapped(sums_own, "smp", d) for d in range(1, n_smp)]
    step = fence(20, step)
    own, message = finish(first, second, [sums_own] + arrived_sums, [step])
    near_b, up_b = down(message), up_two(message)
    others = others_of(own, 1)
    step = fence(20, own)

    whole, part0 = gather(own, others, own, "gather0", [near_a, step])
    got0 = sent(part0)
    near_b, whole = together(near_b, whole)
    far_b = down_again(near_b)
    half = ((samples, width // 2), jnp.bfloat16)
    cols1, near_a, *part1 = call(
        near_body,
        "near",
        [((samples, width), jnp.bfloat16), half] + part_shapes(width),
        [whole, near_a, near_b],
    )
    far_a = down_again(near_a)
    (rows3,) = call(
        assemble_body,
        "rows3",
        [((samples, width), jnp.bfloat16)],
        [up_a, up_b],
        events=[cols1],
    )
    others3 = others_of(rows3, 2)
    panel0 = total(whole, own, got0, "total0", [rows3])
    whole3, part3 = gather(rows3, others3, cols1, "gather3", [fence(3, panel0)], part1)
    got3 = sent(part3)
    part2_b = far_parts(far_b, width // 2, "far_b", [whole3])
    got2_b = sent(part2_b)
    panel3 = total(whole3, cols1, got3, "total3", [fence(12, *part2_b)])
    later = []
    if not shared:
        *part1, panel3 = together(*part1, panel3)
        later = sent(part1, holds)
    part2_a = far_parts(far_a, 0, "far_a", [panel3])
    panel3 = down_two(panel3)
    got2_a = sent(part2_a)
    if shared:
        later = got2_a + got2_b
    ending = total_or_none_body if shared else total_body
    panel2_b = total(whole, far_b, got2_b, "total2b", [*part2_a], ending)
    panel1 = total(
        whole,
        cols1,
        got3 + later,
        "total1",
        [fence(3, panel2_b)],
        functools.partial(total_near_body, n_smp - 1),
    )
    panel2_a = total(whole, far_a, got2_a, "total2a", [panel1], ending)
    return interleave([panel0, panel1, panel2_a, panel2_b, panel3])


def solution(mesh):
    in_specs = (P("smp", ("grp", "var", "sub")), P("smp", ("grp", "var", "sub")))
    out_specs = P(("grp", "var", "smp"), None, "sub")
    return jax.shard_map(
        on_device, mesh=mesh, in_specs=in_specs, out_specs=out_specs, check_vma=False
    )
```

```python
import functools

import jax
import jax.numpy as jnp
from jax import lax
from jax.experimental import pallas as pl
from jax.experimental.pallas import tpu as pltpu
from jax.sharding import PartitionSpec as P

BAND = 4
TAIL = 16
WEIGHTS = {'step1': 40, 'step2': 6, 'step3': 20, 'step4': 3, 'step5': 1, 'step6': 1, 'step7': 25, 'total0': 14, 'gather0': 8, 'total2b': 0, 'total1': 4}


def params(mib):
    return pltpu.CompilerParams(vmem_limit_bytes=mib * 1024 * 1024)


def split3(x):
    high = x.astype(jnp.bfloat16)
    rest = x - high.astype(jnp.float32)
    middle = rest.astype(jnp.bfloat16)
    low = (rest - middle.astype(jnp.float32)).astype(jnp.bfloat16)
    return [high, middle, low]


def encode_body(dosages, observed, first, second, sums, held_d, held_o, sems):
    steps = sems.shape[1]
    samples, width = held_d.shape
    rows = samples // steps
    spans = [pl.ds(i * rows, rows) for i in range(steps)]
    copies = [
        [
            pltpu.make_async_copy(src.at[span], dst.at[span], sems.at[j, i])
            for j, (src, dst) in enumerate(((dosages, held_d), (observed, held_o)))
        ]
        for i, span in enumerate(spans)
    ]
    for pair in copies:
        for copy in pair:
            copy.start()
    parts = [jnp.zeros((8, width), jnp.int32)] * 3
    for span, pair in zip(spans, copies):
        for copy in pair:
            copy.wait()
        weights = held_o[span]
        known = held_d[span] * weights
        code = (known + (weights - 1)).astype(jnp.float32).astype(jnp.bfloat16)
        first[span] = code[:, :first.shape[1]]
        second[span] = code[:, first.shape[1]:]
        for i, part in enumerate((weights, known, known * known)):
            parts[i] += jnp.sum(part.reshape(rows // 8, 8, width), axis=0)
    rows_out = [jnp.sum(p, axis=0, keepdims=True) for p in parts]
    sums[...] = jnp.concatenate(rows_out + [jnp.zeros((5, width), jnp.int32)], axis=0)


def call(body, name, shapes, inputs, mib=32, in_hbm=False, scratch=(), events=()):
    place = pltpu.HBM if in_hbm else pltpu.VMEM
    n = len(inputs)
    skip = len(events)

    def with_events(*refs):
        body(*refs[:n], *refs[n + skip:])

    return pl.pallas_call(
        with_events,
        in_specs=[pl.BlockSpec(memory_space=place)] * n
        + [pl.BlockSpec(memory_space=pl.ANY)] * skip,
        out_specs=[pl.BlockSpec(memory_space=pltpu.VMEM)] * len(shapes),
        out_shape=[jax.ShapeDtypeStruct(shape, kind) for shape, kind in shapes],
        scratch_shapes=scratch,
        compiler_params=params(mib),
        cost_estimate=pl.CostEstimate(
            flops=WEIGHTS.get(name, 0) * 10**9, bytes_accessed=0, transcendentals=0
        ),
        name=name,
    )(*inputs, *events)


def encode(dosages, observed):
    samples, width = dosages.shape
    steps = 8
    cut = width // 2
    return call(
        encode_body,
        "encode",
        [
            ((samples, cut), jnp.bfloat16),
            ((samples, width - cut), jnp.bfloat16),
            ((8, width), jnp.int32),
        ],
        [dosages, observed],
        mib=52,
        in_hbm=True,
        scratch=[
            pltpu.VMEM((samples, width), jnp.int32),
            pltpu.VMEM((samples, width), jnp.int32),
            pltpu.SemaphoreType.DMA((2, steps)),
        ],
    )


def variant_stats(sums):
    counts = jnp.maximum(sums[0], 1)
    n = counts.astype(jnp.float32)
    pivot = jnp.floor(sums[1].astype(jnp.float32) / n + 0.5).astype(jnp.int32)
    rest = (sums[1] - pivot * counts).astype(jnp.float32)
    squares = (sums[2] - 2 * pivot * sums[1] + pivot * pivot * sums[0]).astype(jnp.float32)
    spreads = (squares - rest * rest / n) / n * 1e-4
    means = pivot.astype(jnp.float32) + rest / n
    return means, lax.rsqrt(spreads + 1e-05) * 0.01


def standardize(code, means, scales):
    value = code.astype(jnp.float32)
    return jnp.where(value >= 0, (value - means) * scales, 0.0).astype(jnp.bfloat16)


def finish_body(first, second, *refs):
    sums_refs, (own, message, short, last) = refs[:-4], refs[-4:]
    samples, cut = first.shape
    sums = [sum(r[i:i + 1] for r in sums_refs) for i in range(3)]
    means, scales = variant_stats(sums)
    own[:, :cut] = standardize(first[...], means[:, :cut], scales[:, :cut])
    rest = standardize(second[...], means[:, cut:], scales[:, cut:])
    own[:, cut:] = rest
    message[:samples] = rest
    middle = short.shape[1]
    short[:samples] = rest[:, :middle]
    last[...] = rest[:, middle:]
    rows = split3(means[:, :cut]) + split3(scales[:, :cut])
    none = jnp.zeros((TAIL, cut), jnp.bfloat16)
    message[samples:] = jnp.concatenate(rows + [none[len(rows):]], axis=0)
    spans = [slice(i, i + middle) for i in range(0, cut, middle)]
    rows = [row[:, span] for span in spans for row in rows]
    short[samples:] = jnp.concatenate(rows + [none[len(rows):, :middle]], axis=0)


def finish(first, second, all_sums, events):
    samples, cut = first.shape
    shapes = [
        (samples, 2 * cut),
        (samples + TAIL, cut),
        (samples + TAIL, cut // 2),
        (samples, cut // 2),
    ]
    return call(
        finish_body,
        "finish",
        [(s, jnp.bfloat16) for s in shapes],
        [first, second, *all_sums],
        events=events,
    )


def interleave_body(first, second, third_a, third_b, fourth_a, fourth_b, out):
    tile, width = first.shape
    count = min(tile, 64)
    size = BAND * count
    to_row = lax.broadcasted_iota(jnp.int32, (size, size), 0)
    from_row = lax.broadcasted_iota(jnp.int32, (size, size), 1)
    panel = sum((from_row >= k * count).astype(jnp.int32) for k in range(1, BAND))
    order = (to_row == (from_row - panel * count) * BAND + panel).astype(jnp.float32)
    order = order.astype(jnp.bfloat16)
    for i in range(tile // count):
        span = slice(i * count, (i + 1) * count)
        third = jnp.concatenate([third_a[span], third_b[span]], axis=1)
        fourth = jnp.concatenate([fourth_a[span], fourth_b[span]], axis=1)
        rows = jnp.concatenate([first[span], second[span], third, fourth], axis=0)
        turned = jnp.dot(order, rows, preferred_element_type=jnp.float32)
        out[span] = turned.astype(jnp.bfloat16).reshape(count, BAND, width)


def interleave(panels):
    rows, width = panels[0].shape
    tile = min(rows, 256)
    return pl.pallas_call(
        interleave_body,
        grid=(rows // tile,),
        in_specs=[pl.BlockSpec((tile, p.shape[1]), lambda i: (i, 0)) for p in panels],
        out_specs=pl.BlockSpec((tile, BAND, width), lambda i: (i, 0, 0)),
        out_shape=jax.ShapeDtypeStruct((rows, BAND, width), jnp.bfloat16),
        compiler_params=params(32),
        name="interleave",
    )(*panels)


def product(whole, cols, distance):
    n_smp = lax.axis_size("smp")
    owned = whole.shape[1] // n_smp
    place = lax.rem(lax.axis_index("smp") + distance, n_smp)
    left = whole[:, pl.ds(pl.multiple_of(place * owned, owned), owned)]
    out = lax.dot_general(left, cols, (((0,), (0,)), ((), ())), preferred_element_type=jnp.float32)
    return out * (1.0 / (whole.shape[0] * n_smp))


def send_parts(whole, cols, parts):
    for d, ref in enumerate(parts):
        ref[...] = product(whole, cols, d + 1).astype(jnp.bfloat16)


def holds_three():
    place = lax.axis_index("var")
    return jnp.logical_and(place >= 2, place + 1 < lax.axis_size("var"))


def choose(condition, when_true, when_false):
    pl.when(condition)(when_true)
    pl.when(jnp.logical_not(condition))(when_false)


def copy_parts(spare, parts):
    for source, ref in zip(spare, parts):
        ref[...] = source[...]


def gather_body(n_sub, n_held, n_spare, *refs):
    held, (cols, *rest) = refs[:n_held], refs[n_held:]
    spare, whole, parts = rest[:n_spare], rest[n_spare], rest[n_spare + 1:]
    width = held[0].shape[1]
    pieces = (n_held - 1) // (n_sub - 1)
    count = whole.shape[0] // pieces
    me = lax.axis_index("sub")

    def span(d):
        place = lax.rem(me - d + n_sub, n_sub)
        return pl.ds(pl.multiple_of(place * width, width), width)

    whole[:, span(0)] = held[0][...]
    for d in range(1, n_sub):
        for i in range(pieces):
            whole[i * count:(i + 1) * count, span(d)] = held[1 + (d - 1) * pieces + i][...]
    if not spare:
        send_parts(whole, cols[...], parts)
        return
    cut = parts[0].shape[1]
    for i in range(width // cut):
        span = slice(i * cut, (i + 1) * cut)
        group = parts[i * n_spare:(i + 1) * n_spare]
        choose(
            holds_three(),
            functools.partial(send_parts, whole, cols[:, span], group),
            functools.partial(copy_parts, [r.at[:, span] for r in spare], group),
        )


def from_tail(tail):
    rows = [tail[i:i + 1].astype(jnp.float32) for i in range(6)]
    return (rows[0] + rows[1]) + rows[2], (rows[3] + rows[4]) + rows[5]


def assemble_body(first, message, out):
    samples, cut = first.shape
    out[:, :cut] = standardize(first[...], *from_tail(message[samples:]))
    out[:, cut:] = message[:samples]


def ahead_body(first, short, out):
    samples, width = short.shape[0] - TAIL, short.shape[1]
    for i in range(first.shape[1] // width):
        span = slice(i * width, (i + 1) * width)
        tail = short[samples + 6 * i:samples + 6 * i + 6]
        out[:, span] = standardize(first[:, span], *from_tail(tail))


def near_body(whole, first, short, last, cols, second, *parts):
    cut, width = first.shape[1], short.shape[1]
    second[:, :width] = short[:whole.shape[0]]
    second[:, width:] = last[...]
    cols[:, :cut] = first[...]
    cols[:, cut:] = second[...]
    send_parts(whole, cols[...], parts)


def far_body(begin, n_spare, whole, cols, *refs):
    spare, parts = refs[:n_spare], refs[n_spare:]

    def own():
        send_parts(whole, cols[:whole.shape[0]], parts)

    if not spare:
        own()
        return
    span = slice(begin, begin + cols.shape[1])
    choose(holds_three(), lambda: copy_parts([r.at[:, span] for r in spare], parts), own)


def summed(whole, cols, arrived):
    total = product(whole, cols, 0).astype(jnp.bfloat16).astype(jnp.float32)
    for part in arrived:
        total = total + part.astype(jnp.float32)
    return total.astype(jnp.bfloat16)


def total_body(whole, cols, *refs):
    *arrived, out = refs
    out[...] = summed(whole, cols[:whole.shape[0]], [r[...] for r in arrived])


def total_span_body(begin, whole, cols, *refs):
    total_body(whole, cols.at[:, begin:begin + refs[-1].shape[1]], *refs)


def total_or_none_body(whole, cols, *refs):
    out = refs[-1]

    def none():
        out[...] = jnp.zeros_like(out)

    choose(holds_three(), none, lambda: total_body(whole, cols, *refs))


def total_near_body(n_parts, n_first, whole, cols, *refs):
    first, later, out = refs[:n_first], refs[n_first:-1], refs[-1]

    def total(parts):
        begin = 0
        for i in range(0, len(parts), n_parts):
            group = parts[i:i + n_parts]
            span = slice(begin, begin + group[0].shape[1])
            out[:, span] = summed(whole, cols[:, span], [r[...] for r in group])
            begin = span.stop

    choose(holds_three(), lambda: total(later), lambda: total(first))


def fence_body(*refs):
    refs[-1][...] = jnp.zeros_like(refs[-1])


def fence(weight, *events):
    return pl.pallas_call(
        fence_body,
        in_specs=[pl.BlockSpec(memory_space=pl.ANY)] * len(events),
        out_specs=pl.BlockSpec(memory_space=pltpu.VMEM),
        out_shape=jax.ShapeDtypeStruct((8, 128), jnp.float32),
        compiler_params=params(1),
        cost_estimate=pl.CostEstimate(flops=weight * 10**9, bytes_accessed=0, transcendentals=0),
        name="fence",
    )(*events)


def together(*arrays):
    return lax.optimization_barrier(arrays)


def on_device(dosages, observed):
    n_var = lax.axis_size("var")
    n_smp = lax.axis_size("smp")
    n_sub = lax.axis_size("sub")
    samples, width = dosages.shape
    rows_owned = width * n_sub // n_smp

    def along(x, distance, keep):
        route = [
            (i, i + distance) for i in range(n_var) if 0 <= i + distance < n_var and keep(i)
        ]
        return lax.ppermute(x, "var", route)

    def down(x):
        return along(x, -1, lambda i: True)

    def down_again(x):
        return along(x, -1, lambda i: i + 1 < n_var)

    def up_two(x):
        return along(x, 2, lambda i: i + 3 < n_var)

    def holds(i):
        return i >= 2 and i + 1 < n_var

    shared = not any(holds(i) and i + 2 < n_var for i in range(n_var))

    def down_two(x):
        return along(x, -2, holds)

    def swapped(x, axis, distance, keep=None):
        n = lax.axis_size(axis)
        if keep is None:
            return lax.ppermute(x, axis, [(i, (i + distance) % n) for i in range(n)])
        route = [
            (v * n + i, v * n + (i + distance) % n)
            for v in range(n_var)
            if keep(v)
            for i in range(n)
        ]
        return lax.ppermute(x, ("var", axis), route)

    def others_of(part, pieces):
        count = part.shape[0] // pieces
        cuts = [part[i * count:(i + 1) * count] for i in range(pieces)]
        return [swapped(c, "sub", d) for d in range(1, n_sub) for c in cuts]

    def sent(parts, keep=None):
        return [swapped(p, "smp", d + 1, keep) for d, p in enumerate(parts)]

    def part_shapes(columns):
        return [((rows_owned, columns), jnp.bfloat16)] * (n_smp - 1)

    def gather(part, others, cols, name, events, spare=()):
        block = ((samples, width * n_sub), jnp.bfloat16)
        body = functools.partial(gather_body, n_sub, 1 + len(others), len(spare))
        shapes = [block] + (part_shapes(width // 2) * 2 if spare else part_shapes(width))
        inputs = [part, *others, cols, *spare]
        whole, *parts = call(body, name, shapes, inputs, events=events)
        return whole, parts

    def far_parts(cols, begin, name, events):
        spare = part1 if shared else []
        body = functools.partial(far_body, begin, len(spare))
        return call(body, name, part_shapes(width // 2), [whole, cols, *spare], events=events)

    def total(whole, cols, arrived, name, events, body=total_body):
        shape = ((rows_owned, cols.shape[1]), jnp.bfloat16)
        return call(body, name, [shape], [whole, cols, *arrived], events=events)[0]

    first, second, sums_own = encode(dosages, observed)
    near_a = down(first)
    step = fence(WEIGHTS["step1"], first)
    sums_own, first_up, step = together(sums_own, first, step)
    up_a = up_two(first_up)
    arrived_sums = [swapped(sums_own, "smp", d) for d in range(1, n_smp)]
    step = fence(WEIGHTS["step2"], step)
    own, message, short, last = finish(first, second, [sums_own] + arrived_sums, [step])
    near_b, up_b = down(short), up_two(message)
    others = others_of(own, 1)
    step = fence(WEIGHTS["step3"], own)
    last, *others = together(last, *others)
    near_c = down(last)

    whole, part0 = gather(own, others, own, "gather0", [near_a, step])
    got0 = sent(part0)
    near_b, whole = together(near_b, whole)
    half = ((samples, width // 2), jnp.bfloat16)
    (near_a,) = call(ahead_body, "ahead", [half], [near_a, near_b])
    far_a = down_again(near_a)
    near_c, near_a = together(near_c, near_a)
    cols1, second, *part1 = call(
        near_body,
        "near",
        [((samples, width), jnp.bfloat16), half] + part_shapes(width),
        [whole, near_a, near_b, near_c],
    )
    far_b = down_again(second)
    (rows3,) = call(
        assemble_body,
        "rows3",
        [((samples, width), jnp.bfloat16)],
        [up_a, up_b],
        events=[cols1],
    )
    others3 = others_of(rows3, 2)
    panel0 = total(whole, own, got0, "total0", [rows3])
    whole3, part3 = gather(rows3, others3, cols1, "gather3", [fence(WEIGHTS["step4"], panel0)], part1)
    count = n_smp - 1
    got3 = [sent(part3[:count]), sent(part3[count:])]
    part2_a = far_parts(far_a, 0, "far_a", [whole3])
    got2_a = sent(part2_a)
    panel3 = []
    step = fence(WEIGHTS["step5"], *part2_a)
    for i in range(2):
        shape = ((rows_owned, width // 2), jnp.bfloat16)
        body = functools.partial(total_span_body, i * (width // 2))
        (panel,) = call(body, "total3", [shape], [whole3, cols1, *got3[i]], events=[step])
        step = fence(WEIGHTS["step6"], panel)
        panel3.append(down_two(panel))
    later = []
    if not shared:
        *part1, step = together(*part1, step)
        later = sent(part1, holds)
    part2_b = far_parts(far_b, width // 2, "far_b", [step])
    got2_b = sent(part2_b)
    if shared:
        later = got2_a + got2_b
    ending = total_or_none_body if shared else total_body
    panel2_a = total(whole, far_a, got2_a, "total2a", [*part2_b], ending)
    panel1 = total(
        whole,
        cols1,
        got3[0] + got3[1] + later,
        "total1",
        [fence(WEIGHTS["step7"], panel2_a)],
        functools.partial(total_near_body, count, 2 * count),
    )
    panel2_b = total(whole, far_b, got2_b, "total2b", [panel1], ending)
    return interleave([panel0, panel1, panel2_a, panel2_b, *panel3])


def solution(mesh):
    in_specs = (P("smp", ("grp", "var", "sub")), P("smp", ("grp", "var", "sub")))
    out_specs = P(("grp", "var", "smp"), None, "sub")
    return jax.shard_map(
        on_device, mesh=mesh, in_specs=in_specs, out_specs=out_specs, check_vma=False
    )
```
